32 devices in a mesh: grp: 2 (over x), blk: 8 (over z, y), face: 2 (over core).
Axes of the slice: x: 2, y: 2, z: 4, core: 2. Of those that a mesh axis runs over, the one named last changes fastest.
Arguments:
- record: float32 [8192, 4096], P('blk', ('grp', 'face')), parts along dimension 1
- face_area: int32 [2048], P('face'), may hold values from 4 to 64
- face_tap: int32 [2048], P('face'), may hold values from 0 to 511
- lever_table: int32 [512, 3], replicated, may hold values from -4 to 4
- start_modes: float32 [2, 16, 16, 4], replicated, may hold values from -6 to 6
Outputs:
- cross_spectra: float32 [2, 32, 16, 16], P(None, 'grp', 'blk'), parts along dimension 1
- modal_forces: float32 [2, 32, 4, 3], P(None, 'grp'), parts along dimension 1
The draws below stay inside these ranges and needn't reach their ends.
There are 2 independent parts, one for each index of `grp`. The reference program is written for one: setup_inputs(seed, part) draws one part's arguments, and reference() takes and returns one part's arrays. A program takes and returns all parts, laid end to end along the dimension named above; an argument that names none is the same for every part. Nothing has to cross between parts.
All inputs are finite; a program needn't handle non-finite values.
Results may differ from the reference program's by a relative error of at most 0.0001.
Values sent between devices are 32-bit elements; how exact they have to be, the bound alone decides.
No kernel may reach another device: no remote copies, remote signals or barrier semaphores. Data moves between devices by JAX's collectives and lax.ppermute only.
A program may use at most 64 MiB of HBM per device.

```python
import math
import jax
import jax.numpy as jnp
from jax import lax

NFFT = 1024
HOP = 512
BIN = 16
FIRST_BIN = 24
NMODE = 4
PITERS = 2
NB = 16
FACES = 2048
NTAP = 512
NC = 3


tone_count = 6


def draw_record(key, part):
    keys = jax.random.split(key, 4)
    total_steps = NB * HOP
    noise = jax.random.normal(keys[0], (total_steps, FACES), jnp.float32)
    tone_bins = FIRST_BIN + jax.random.randint(keys[1], (tone_count,), 0, BIN)
    amplitude = 0.12 * jax.random.normal(keys[2], (tone_count, FACES), jnp.float32)
    phase = jax.random.uniform(keys[3], (tone_count, FACES), jnp.float32, 0.0, 2.0 * math.pi)
    steps = jnp.arange(total_steps, dtype=jnp.int32)
    signal = noise
    for tone_index in range(tone_count):
        angle = (steps * tone_bins[tone_index] % NFFT).astype(jnp.float32) * (2.0 * math.pi / NFFT)
        signal = signal + amplitude[tone_index][None, :] * jnp.cos(angle[:, None] + phase[tone_index][None, :])
    return signal


def with_ends(entries, own_key, low, largest):
    place = [jax.random.randint(jax.random.fold_in(own_key, axis), (), 0, length) for axis, length in enumerate(entries.shape)]
    widest = entries.shape.index(max(entries.shape))
    beside = place[:widest] + [(place[widest] + 1) % entries.shape[widest]] + place[widest + 1:]
    return entries.at[tuple(place)].set(low).at[tuple(beside)].set(largest)


def normal_values(key, dims, width, limit, kind=jnp.bfloat16):
    return jnp.clip(width * jax.random.normal(key, dims, jnp.float32), -limit, limit).astype(kind)


def setup_inputs(seed: int = 0, part: int = 0) -> dict:
    key_of = jax.random.split(jax.random.key(seed), 6)
    part_keys = jax.random.split(jax.random.fold_in(key_of[5], part), 6)
    return {
        "record": draw_record(jax.random.fold_in(jax.random.fold_in(key_of[5], part), 71), part),
        "face_area": with_ends(jax.random.randint(key_of[1], (FACES,), 4, 65), jax.random.fold_in(key_of[1], 1), 4, 64).astype(jnp.int32),
        "face_tap": with_ends(jax.random.randint(key_of[2], (FACES,), 0, NTAP), jax.random.fold_in(key_of[2], 1), 0, NTAP - 1).astype(jnp.int32),
        "lever_table": with_ends(jax.random.randint(key_of[3], (NTAP, NC), -4, 5), jax.random.fold_in(key_of[3], 1), -4, 4).astype(jnp.int32),
        "start_modes": normal_values(key_of[4], (2, BIN, NB, NMODE), 1.0, 6.0, jnp.float32),
    }


HIGH = lax.Precision.HIGHEST

def band_twiddle():
    steps = jnp.arange(NFFT, dtype=jnp.int32)
    bins = FIRST_BIN + jnp.arange(BIN, dtype=jnp.int32)
    angle = (steps[:, None] * bins[None, :] % NFFT).astype(jnp.float32) * (2.0 * math.pi / NFFT)
    window = 0.5 - 0.5 * jnp.cos(steps.astype(jnp.float32) * (2.0 * math.pi / NFFT))
    scaling = jnp.sqrt(jnp.sum(window * window))
    cosine = window[:, None] * jnp.cos(angle) / scaling
    sine = -window[:, None] * jnp.sin(angle) / scaling
    return jnp.concatenate([cosine, sine], axis=1)

def reference(record, face_area, face_tap, lever_table, start_modes):
    twiddle = band_twiddle()
    halves = record.reshape(NB, HOP, FACES)
    following = jnp.roll(halves, -1, axis=0)
    spectra = jnp.einsum('tk,btf->kbf', twiddle[:HOP], halves, precision=HIGH)
    spectra = spectra + jnp.einsum('tk,btf->kbf', twiddle[HOP:], following, precision=HIGH)
    real_part = spectra[:BIN]
    imag_part = spectra[BIN:]
    weight = face_area.astype(jnp.float32) / 64.0
    gram_re = jnp.einsum('kif,kjf->kij', real_part * weight, real_part, precision=HIGH)
    gram_re = gram_re + jnp.einsum('kif,kjf->kij', imag_part * weight, imag_part, precision=HIGH)
    gram_im = jnp.einsum('kif,kjf->kij', real_part * weight, imag_part, precision=HIGH)
    gram_im = gram_im - jnp.einsum('kif,kjf->kij', imag_part * weight, real_part, precision=HIGH)
    gram_re = gram_re / FACES
    gram_im = gram_im / FACES
    modes_re = start_modes[0]
    modes_im = start_modes[1]
    for sweep_index in range(PITERS):
        new_re = jnp.einsum('kij,kjm->kim', gram_re, modes_re, precision=HIGH) - jnp.einsum('kij,kjm->kim', gram_im, modes_im, precision=HIGH)
        new_im = jnp.einsum('kij,kjm->kim', gram_re, modes_im, precision=HIGH) + jnp.einsum('kij,kjm->kim', gram_im, modes_re, precision=HIGH)
        column_scale = jnp.sqrt(lax.optimization_barrier(jnp.sum(new_re * new_re + new_im * new_im, axis=1, keepdims=True)) / NB + 1e-06)
        modes_re = new_re / column_scale
        modes_im = new_im / column_scale
    onehot = (face_tap[:, None] == jnp.arange(NTAP, dtype=jnp.int32)[None, :]).astype(jnp.float32)
    face_weight = weight[:, None] * jnp.dot(onehot, lever_table.astype(jnp.float32), precision=HIGH)
    force_norm = math.sqrt(FACES * NB)
    load_re = jnp.einsum('kbf,fc->kbc', real_part, face_weight, precision=HIGH) / force_norm
    load_im = jnp.einsum('kbf,fc->kbc', imag_part, face_weight, precision=HIGH) / force_norm
    force_re = jnp.einsum('kbc,kbm->kmc', load_re, modes_re, precision=HIGH) - jnp.einsum('kbc,kbm->kmc', load_im, modes_im, precision=HIGH)
    force_im = jnp.einsum('kbc,kbm->kmc', load_re, modes_im, precision=HIGH) + jnp.einsum('kbc,kbm->kmc', load_im, modes_re, precision=HIGH)
    return (jnp.stack([gram_re, gram_im]), jnp.stack([force_re, force_im]))
```

```python
import functools
import math

import jax
import jax.numpy as jnp
import ml_dtypes
import numpy as np
from jax import lax
from jax.experimental import pallas as pl
from jax.experimental.pallas import tpu as pltpu
from jax.sharding import PartitionSpec as P

NFFT = 1024
HOP = 512
BIN = 16
FIRST_BIN = 24
PITERS = 2
BLK_DEV = 2
NTAP = 512
NMODE = 4
NC = 3
ROWS = 8
F_LANE = 64

HIGH = lax.Precision.HIGHEST
NT = (((1,), (1,)), ((), ()))


def band_twiddle():
    steps = np.arange(NFFT)
    bins = FIRST_BIN + np.arange(BIN)
    angle = (steps[:, None] * bins[None, :] % NFFT) * (2.0 * math.pi / NFFT)
    window = 0.5 - 0.5 * np.cos(steps * (2.0 * math.pi / NFFT))
    scaling = np.sqrt(np.sum(window * window))
    cosine = window[:, None] * np.cos(angle) / scaling
    sine = -window[:, None] * np.sin(angle) / scaling
    return np.concatenate([cosine, sine], axis=1).astype(np.float32)


def thirds(x, cast):
    first = x.astype(jnp.bfloat16)
    rest = x - cast(first)
    second = rest.astype(jnp.bfloat16)
    third = (rest - cast(second)).astype(jnp.bfloat16)
    return first, second, third


def message_twiddle():
    twiddle = band_twiddle()
    early, late = twiddle[:HOP].T.reshape(2, BIN, HOP), twiddle[HOP:].T.reshape(2, BIN, HOP)
    rows = np.zeros((BIN, ROWS, 2, HOP), np.float32)
    for part in range(2):
        rows[:, part, 0] = early[part]
        rows[:, part, 1] = late[part]
        rows[:, 2 + part, 1] = early[part]
        rows[:, 4 + part, 0] = late[part]
    rows = rows.reshape(BIN * ROWS, NFFT)
    first = rows.astype(ml_dtypes.bfloat16)
    rest = rows - first.astype(np.float32)
    second = rest.astype(ml_dtypes.bfloat16)
    third = (rest - second.astype(np.float32)).astype(ml_dtypes.bfloat16)
    return np.concatenate([first, second, third], axis=0)


def f32(x):
    return x.astype(jnp.float32)


def spectra_kernel(odd_ref, twiddle_ref, record_ref, area_ref, tap_ref, lever_ref, out_ref):
    m = BIN * ROWS
    first, second, third = thirds(record_ref[...], f32)
    dot = functools.partial(jnp.dot, preferred_element_type=jnp.float32)
    one = dot(twiddle_ref[...], first)
    two = dot(twiddle_ref[: 2 * m], second)
    three = dot(twiddle_ref[:m], third)
    spectra = ((one[2 * m :] + two[m:]) + three) + (one[m : 2 * m] + two[:m]) + one[:m]
    root = jnp.sqrt(f32(area_ref[...]) / 64.0)
    faces = root.shape[1]
    taps = lax.broadcasted_iota(jnp.int32, (NTAP, faces), 0)
    onehot = jnp.where(taps == tap_ref[...], 1.0, 0.0).astype(jnp.bfloat16)
    lever = f32(lever_ref[...]).astype(jnp.bfloat16)
    force = dot(lever, onehot) * root
    odd = odd_ref[0] != 0
    pair = jnp.where(odd, force[2:4], force[0:2])
    out_ref[...] = (spectra * root).reshape(BIN, ROWS, faces)
    out_ref[:, 6:8, :] = jnp.broadcast_to(pair[None], (BIN, 2, faces))


def spectra_call(odd, twiddle, record, area, tap, lever, chunk=256):
    steps, faces = record.shape
    return pl.pallas_call(
        spectra_kernel,
        grid=(faces // chunk,),
        in_specs=[
            pl.BlockSpec(memory_space=pltpu.SMEM),
            pl.BlockSpec(twiddle.shape, lambda i: (0, 0)),
            pl.BlockSpec((steps, chunk), lambda i: (0, i)),
            pl.BlockSpec((1, chunk), lambda i: (0, i)),
            pl.BlockSpec((1, chunk), lambda i: (0, i)),
            pl.BlockSpec(lever.shape, lambda i: (0, 0)),
        ],
        out_specs=pl.BlockSpec((BIN, ROWS, chunk), lambda i: (0, 0, i)),
        out_shape=jax.ShapeDtypeStruct((BIN, ROWS, faces), jnp.float32),
        compiler_params=pltpu.CompilerParams(vmem_limit_bytes=32 * 2**20),
        name="band_spectra",
    )(odd, twiddle, record, area, tap, lever)


def modes_kernel(total_faces, block_count, bin_ref, got_ref, start_ref, out_ref):
    cycle = block_count // BLK_DEV
    dot = functools.partial(lax.dot_general, preferred_element_type=jnp.float32)
    real, imag, force = [], [], []
    for face in range(2):
        got = [got_ref[2 * d + face] for d in range(cycle)]
        rows = ([], [])
        for d in range(cycle):
            for part in range(2):
                rows[part].append(got[d][part : part + 1])
                rows[part].append(got[d][2 + part : 3 + part] + got[(d + 1) % cycle][4 + part : 5 + part])
        real.append(jnp.concatenate(rows[0], axis=0))
        imag.append(jnp.concatenate(rows[1], axis=0))
        force.append(jnp.concatenate([got[0][6:8], got[1][6:7], jnp.zeros_like(got[0][:5])], axis=0))
    real = jnp.concatenate(real, axis=1)
    imag = jnp.concatenate(imag, axis=1)
    force = jnp.concatenate(force, axis=1)
    q = jnp.concatenate([real, imag], axis=0)
    both = dot(jnp.concatenate([q, force], axis=0), q, NT, precision=HIGH)
    n = block_count
    rr, ri = both[:n, :n], both[:n, n : 2 * n]
    ir, ii = both[n : 2 * n, :n], both[n : 2 * n, n : 2 * n]
    gram_re = (rr + ii) / total_faces
    gram_im = (ri - ir) / total_faces
    gram = jnp.concatenate(
        [jnp.concatenate([gram_re, -gram_im], axis=1), jnp.concatenate([gram_im, gram_re], axis=1)], axis=0
    )
    load = both[2 * n :] / math.sqrt(total_faces * block_count)
    own = bin_ref[0]
    modes = jnp.concatenate([start_ref[0, own], start_ref[1, own]], axis=1)
    for _ in range(PITERS):
        new = dot(modes, gram, (((1,), (0,)), ((), ())), precision=HIGH)
        scale = jnp.sqrt(jnp.sum(new * new, axis=1, keepdims=True) / block_count + 1e-06)
        modes = new / scale
    re, im = modes[:, :n], modes[:, n:]
    signed = jnp.concatenate(
        [jnp.concatenate([re, -im], axis=1), jnp.concatenate([im, re], axis=1)], axis=0
    )
    padded = jnp.concatenate([jnp.zeros((F_LANE, 2 * n), jnp.float32), load, jnp.zeros((128 - F_LANE - 8, 2 * n), jnp.float32)], axis=0)
    reply = dot(signed, padded, NT, precision=HIGH)
    for d in range(cycle):
        for face in range(2):
            out_ref[2 * d + face] = reply
            out_ref[2 * d + face, 0:2, 0 : 2 * n] = gram[n + 2 * d : n + 2 * d + 2]


def modes_call(own_bin, got, start, total_faces, block_count):
    return pl.pallas_call(
        functools.partial(modes_kernel, total_faces, block_count),
        in_specs=[pl.BlockSpec(memory_space=pltpu.SMEM), pl.BlockSpec(memory_space=pltpu.VMEM), pl.BlockSpec(memory_space=pltpu.VMEM)],
        out_specs=pl.BlockSpec(memory_space=pltpu.VMEM),
        out_shape=jax.ShapeDtypeStruct((BIN, 8, 128), jnp.float32),
        compiler_params=pltpu.CompilerParams(vmem_limit_bytes=32 * 2**20),
        name="bin_modes",
    )(own_bin, got, start)


def by_bins(record, face_area, face_tap, lever_table, start_modes):
    faces = record.shape[1]
    cycle = lax.axis_size("blk")
    block_count = BLK_DEV * cycle
    place = lax.axis_index("blk")
    odd = jnp.reshape(place % 2, (1,)).astype(jnp.int32)
    own_bin = jnp.reshape(2 * place + lax.axis_index("face"), (1,)).astype(jnp.int32)
    lever = jnp.pad(lever_table.T, ((0, 8 - NC), (0, 0)))
    messages = spectra_call(
        odd, jnp.asarray(message_twiddle()), record, face_area.reshape(1, faces), face_tap.reshape(1, faces), lever
    )
    got = lax.all_to_all(messages, ("blk", "face"), 0, 0, tiled=True)
    replies = modes_call(own_bin, got, start_modes.transpose(0, 1, 3, 2), faces * 2, block_count)
    back = lax.all_to_all(replies, ("blk", "face"), 0, 0, tiled=True)
    n = block_count
    gram_rows = jnp.stack([back[:, 0:2, n : 2 * n], back[:, 0:2, 0:n]])
    forces = jnp.stack([back[:, 0:4, F_LANE : F_LANE + NC], back[:, 4:8, F_LANE : F_LANE + NC]])
    return gram_rows, forces


def shifted(x, axis, by):
    count = lax.axis_size(axis)
    return lax.ppermute(x, axis, [(i, (i + by) % count) for i in range(count)])


def gram_tiles(weighted, others):
    real_tile = jnp.einsum("kif,kjf->kij", weighted[0], others[0], precision=HIGH)
    real_tile = real_tile + jnp.einsum("kif,kjf->kij", weighted[1], others[1], precision=HIGH)
    imag_tile = jnp.einsum("kif,kjf->kij", weighted[0], others[1], precision=HIGH)
    imag_tile = imag_tile - jnp.einsum("kif,kjf->kij", weighted[1], others[0], precision=HIGH)
    return jnp.stack([real_tile, imag_tile])


def by_rows(record, face_area, face_tap, lever_table, start_modes):
    faces = record.shape[1]
    cycle = lax.axis_size("blk")
    block_count = BLK_DEV * cycle
    total_faces = faces * lax.axis_size("face")
    twiddle = jnp.asarray(band_twiddle())
    hops = record.reshape(BLK_DEV, HOP, faces)
    early = jnp.einsum("tk,btf->kbf", twiddle[:HOP], hops, precision=HIGH)
    late = jnp.einsum("tk,btf->kbf", twiddle[HOP:], hops, precision=HIGH)
    following = shifted(late[:, :1], "blk", -1)
    spectra = early + jnp.concatenate([late[:, 1:], following], axis=1)
    panels = jnp.stack([spectra[:BIN], spectra[BIN:]])
    weight = face_area.astype(jnp.float32) / 64.0
    gram_rows = gram_tiles(panels * weight, lax.all_gather(panels, "blk", axis=2, tiled=True))
    gram_rows = lax.psum(gram_rows, "face") / total_faces
    gram = lax.all_gather(gram_rows, "blk", axis=2, tiled=True)
    re, im = start_modes[0], start_modes[1]
    product = functools.partial(jnp.einsum, "kij,kjm->kim", precision=HIGH)
    for _ in range(PITERS):
        re, im = product(gram[0], re) - product(gram[1], im), product(gram[0], im) + product(gram[1], re)
        scale = jnp.sqrt(jnp.sum(re * re + im * im, axis=1, keepdims=True) / block_count + 1e-06)
        re, im = re / scale, im / scale
    own = BLK_DEV * lax.axis_index("blk")
    re = lax.dynamic_slice_in_dim(re, own, BLK_DEV, 1)
    im = lax.dynamic_slice_in_dim(im, own, BLK_DEV, 1)
    onehot = (face_tap[:, None] == jnp.arange(NTAP, dtype=jnp.int32)[None, :]).astype(jnp.float32)
    face_weight = weight[:, None] * jnp.dot(onehot, lever_table.astype(jnp.float32), precision=HIGH)
    load = jnp.einsum("pkbf,fc->pkbc", panels, face_weight, precision=HIGH) / math.sqrt(total_faces * block_count)
    force = functools.partial(jnp.einsum, "kbc,kbm->kmc", precision=HIGH)
    forces = jnp.stack([force(load[0], re) - force(load[1], im), force(load[0], im) + force(load[1], re)])
    return gram_rows, lax.psum(forces, ("blk", "face"))


def solution(mesh):
    fits = mesh.shape["blk"] * mesh.shape["face"] == BIN and mesh.shape["face"] == 2
    return jax.shard_map(
        by_bins if fits else by_rows,
        mesh=mesh,
        in_specs=(P("blk", ("grp", "face")), P("face"), P("face"), P(), P()),
        out_specs=(P(None, "grp", "blk", None), P(None, "grp", None, None)),
        check_vma=False,
    )
```

```python
import functools
import math

import jax
import jax.numpy as jnp
import ml_dtypes
import numpy as np
from jax import lax
from jax.experimental import pallas as pl
from jax.experimental.pallas import tpu as pltpu
from jax.sharding import PartitionSpec as P

NFFT = 1024
HOP = 512
BIN = 16
FIRST_BIN = 24
PITERS = 2
BLK_DEV = 2
NTAP = 512
NMODE = 4
NC = 3
LANES = 128
SPANS = 8
ROWS = 48
SPLIT = 4
F_LANE = 64
VMEM_LIMIT = 60 * 2**20

HIGH = lax.Precision.HIGHEST
NT = (((1,), (1,)), ((), ()))


def band_twiddle():
    steps = np.arange(NFFT)
    bins = FIRST_BIN + np.arange(BIN)
    angle = (steps[:, None] * bins[None, :] % NFFT) * (2.0 * math.pi / NFFT)
    window = 0.5 - 0.5 * np.cos(steps * (2.0 * math.pi / NFFT))
    scaling = np.sqrt(np.sum(window * window))
    cosine = window[:, None] * np.cos(angle) / scaling
    sine = -window[:, None] * np.sin(angle) / scaling
    return np.concatenate([cosine, sine], axis=1).astype(np.float32)


def thirds(x, cast):
    first = x.astype(jnp.bfloat16)
    rest = x - cast(first)
    second = rest.astype(jnp.bfloat16)
    third = (rest - cast(second)).astype(jnp.bfloat16)
    return first, second, third


def folded_twiddle():
    twiddle = band_twiddle().reshape(2, HOP, 2, BIN)
    rows = twiddle.transpose(0, 3, 2, 1).reshape(4 * BIN, HOP)
    first = rows.astype(ml_dtypes.bfloat16)
    rest = rows - first.astype(np.float32)
    second = rest.astype(ml_dtypes.bfloat16)
    third = (rest - second.astype(np.float32)).astype(ml_dtypes.bfloat16)
    return np.concatenate([first, second, third], axis=0)


def f32(x):
    return x.astype(jnp.float32)


def even_row(span):
    return 2 * span


def odd_row(span):
    return ROWS // 2 + 2 * span


def late_row(span):
    return 2 * SPANS + 2 * span if span < SPANS // 2 else ROWS // 2 + SPANS + 2 * span


def spectra_kernel(
    twiddle_hbm, record_hbm, area_hbm, tap_hbm, lever_hbm, out_ref, force_ref, twiddle, record, area, tap, lever, sems, record_sems
):
    faces = record.shape[1]
    width = faces // SPLIT
    small = [
        pltpu.make_async_copy(source, target, sems.at[i])
        for i, (source, target) in enumerate(((area_hbm, area), (tap_hbm, tap), (lever_hbm, lever), (twiddle_hbm, twiddle)))
    ]
    parts = [slice(q * width, (q + 1) * width) for q in range(SPLIT)]
    large = [
        pltpu.make_async_copy(record_hbm.at[:, part], record.at[:, part], record_sems.at[q]) for q, part in enumerate(parts)
    ]
    for copy in small[:3]:
        copy.start()
    small[3].start()
    for copy in large:
        copy.start()
    for copy in small[:3]:
        copy.wait()
    dot = functools.partial(jnp.dot, preferred_element_type=jnp.float32)
    root = jnp.sqrt(f32(area[...]) / 64.0)
    taps = lax.broadcasted_iota(jnp.int32, (NTAP, faces), 0)
    onehot = jnp.where(taps == tap[...], 1.0, 0.0).astype(jnp.bfloat16)
    force_ref[0:NC] = dot(f32(lever[...]).astype(jnp.bfloat16), onehot) * root
    force_ref[NC:] = jnp.zeros((8 - NC, faces), jnp.float32)
    small[3].wait()
    m = 4 * BIN
    for q, part in enumerate(parts):
        large[q].wait()
        halves = []
        for hop in range(BLK_DEV):
            first, second, third = thirds(record[hop * HOP : (hop + 1) * HOP, part], f32)
            one = dot(twiddle[...], first)
            two = dot(twiddle[: 2 * m], second)
            three = dot(twiddle[:m], third)
            halves.append((((one[2 * m :] + two[m:]) + three) + (one[m : 2 * m] + two[:m]) + one[:m]) * root[:, part])
        even = halves[0][: 2 * BIN] + halves[1][2 * BIN :]
        odd = halves[1][: 2 * BIN]
        late = halves[0][2 * BIN :]
        for k in range(BIN):
            pair = slice(2 * k, 2 * k + 2)
            for i in range(width // LANES):
                span, lane = q * (width // LANES) + i, slice(i * LANES, (i + 1) * LANES)
                out_ref[k, even_row(span) : even_row(span) + 2, :] = even[pair, lane]
                out_ref[k, odd_row(span) : odd_row(span) + 2, :] = odd[pair, lane]
                out_ref[k, late_row(span) : late_row(span) + 2, :] = late[pair, lane]


def spectra_call(twiddle, record, area, tap, lever):
    steps, faces = record.shape
    return pl.pallas_call(
        spectra_kernel,
        in_specs=[pl.BlockSpec(memory_space=pl.ANY)] * 5,
        out_specs=[pl.BlockSpec(memory_space=pltpu.VMEM)] * 2,
        out_shape=[
            jax.ShapeDtypeStruct((BIN, ROWS, LANES), jnp.float32),
            jax.ShapeDtypeStruct((8, faces), jnp.float32),
        ],
        scratch_shapes=[
            pltpu.VMEM(twiddle.shape, jnp.bfloat16),
            pltpu.VMEM(record.shape, jnp.float32),
            pltpu.VMEM((1, faces), jnp.int32),
            pltpu.VMEM((1, faces), jnp.int32),
            pltpu.VMEM(lever.shape, jnp.int32),
            pltpu.SemaphoreType.DMA((4,)),
            pltpu.SemaphoreType.DMA((SPLIT,)),
        ],
        compiler_params=pltpu.CompilerParams(vmem_limit_bytes=VMEM_LIMIT),
        name="band_spectra",
    )(twiddle, record, area, tap, lever)


def modes_kernel(total_faces, block_count, place_ref, got_ref, own_force_ref, other_force_ref, start_ref, out_ref):
    n = block_count
    dot = functools.partial(lax.dot_general, preferred_element_type=jnp.float32)
    is_odd = lax.broadcasted_iota(jnp.int32, (n, LANES), 0) % 2 == 1
    columns = []
    for face in range(2):
        base = face * (n // BLK_DEV) * ROWS
        for span in range(SPANS):
            rows = []
            for part in range(2):
                direct = got_ref[pl.ds(base + even_row(span) + part, n, stride=ROWS // 2), :]
                start = late_row(span) + part
                shift = 1 if start < ROWS // 2 else 2
                late = got_ref[pl.ds(base + start % (ROWS // 2), n, stride=ROWS // 2), :]
                rows.append(direct + jnp.where(is_odd, pltpu.roll(late, n - shift, 0), 0.0))
            columns.append(jnp.concatenate(rows, axis=0))
    q_all = jnp.concatenate(columns, axis=1)
    face_one = place_ref[1] != 0
    own, other = own_force_ref[...], other_force_ref[...]
    force = jnp.concatenate([jnp.where(face_one, other, own), jnp.where(face_one, own, other)], axis=1)
    spectra = jnp.concatenate(thirds(q_all, f32), axis=0)
    forces = jnp.concatenate(thirds(jnp.concatenate([force, jnp.zeros_like(force)], axis=0), f32), axis=0)
    both = dot(jnp.concatenate([spectra, forces], axis=0), spectra, NT)
    m = 2 * n
    both = (both[:, 2 * m : 3 * m] + both[:, m : 2 * m]) + both[:, :m]
    square = (both[2 * m : 3 * m] + both[m : 2 * m]) + both[:m]
    load = (both[3 * m + 32 : 3 * m + 40] + both[3 * m + 16 : 3 * m + 24]) + both[3 * m : 3 * m + 8]
    gram_re = (square[:n, :n] + square[n:, n:]) / total_faces
    gram_im = (square[:n, n:] - square[n:, :n]) / total_faces
    gram = jnp.concatenate(
        [jnp.concatenate([gram_re, -gram_im], axis=1), jnp.concatenate([gram_im, gram_re], axis=1)], axis=0
    )
    load = load / math.sqrt(total_faces * block_count)
    modes = jnp.concatenate([start_ref[0, place_ref[0]], start_ref[1, place_ref[0]]], axis=1)
    for _ in range(PITERS):
        new = dot(modes, gram, (((1,), (0,)), ((), ())), precision=HIGH)
        scale = jnp.sqrt(jnp.sum(new * new, axis=1, keepdims=True) / block_count + 1e-06)
        modes = new / scale
    re, im = modes[:, :n], modes[:, n:]
    signed = jnp.concatenate([jnp.concatenate([re, -im], axis=1), jnp.concatenate([im, re], axis=1)], axis=0)
    blank = jnp.zeros((F_LANE, 2 * n), jnp.float32)
    padded = jnp.concatenate([blank, signed, blank[: 128 - F_LANE - 2 * NMODE]], axis=0)
    answer = dot(load, padded, NT, precision=HIGH)
    tail = answer[0:1] + pltpu.roll(answer[1:2], 2 * NMODE, 1) + pltpu.roll(answer[2:3], 4 * NMODE, 1)
    lower = jnp.concatenate([gram[n:], jnp.zeros((n, 128 - m), jnp.float32)], axis=1)
    moved = pltpu.roll(lower, m, 1)
    for d in range(n // BLK_DEV):
        reply = lower[2 * d : 2 * d + 1] + moved[2 * d + 1 : 2 * d + 2] + tail
        for face in range(2):
            out_ref[face * (n // BLK_DEV) + d] = reply


def modes_call(place, got, own_force, other_force, start, total_faces, block_count):
    vmem = pl.BlockSpec(memory_space=pltpu.VMEM)
    return pl.pallas_call(
        functools.partial(modes_kernel, total_faces, block_count),
        in_specs=[pl.BlockSpec(memory_space=pltpu.SMEM), vmem, vmem, vmem, vmem],
        out_specs=vmem,
        out_shape=jax.ShapeDtypeStruct((BIN, 1, 128), jnp.float32),
        compiler_params=pltpu.CompilerParams(vmem_limit_bytes=32 * 2**20),
        name="bin_modes",
    )(place, got, own_force, other_force, start)


def outputs_kernel(block_count, back_ref, gram_ref, forces_ref):
    n = block_count
    back = back_ref[...]
    for part in range(2):
        for row in range(BLK_DEV):
            lane = 2 * n * row + n * (1 - part)
            gram_ref[part, :, row, :] = back[:, lane : lane + n]
    turned = back.T
    for part in range(2):
        for c in range(NC):
            line = F_LANE + 2 * NMODE * c + NMODE * part
            forces_ref[part, c] = turned[line : line + NMODE]


def outputs_call(back, block_count):
    vmem = pl.BlockSpec(memory_space=pltpu.VMEM)
    return pl.pallas_call(
        functools.partial(outputs_kernel, block_count),
        in_specs=[vmem],
        out_specs=[vmem, vmem],
        out_shape=[
            jax.ShapeDtypeStruct((2, BIN, BLK_DEV, block_count), jnp.float32),
            jax.ShapeDtypeStruct((2, NC, NMODE, BIN), jnp.float32),
        ],
        name="outputs",
    )(back)


def by_bins(record, face_area, face_tap, lever_table, start_modes):
    faces = record.shape[1]
    cycle = lax.axis_size("blk")
    block_count = BLK_DEV * cycle
    face = lax.axis_index("face")
    place = jnp.stack([cycle * face + lax.axis_index("blk"), face]).astype(jnp.int32)
    messages, force = spectra_call(
        jnp.asarray(folded_twiddle()), record, face_area.reshape(1, faces), face_tap.reshape(1, faces), lever_table.T
    )
    other_force = shifted(force, "face", 1)
    got = lax.all_to_all(messages, ("face", "blk"), 0, 0, tiled=True)
    replies = modes_call(
        place, got.reshape(BIN * ROWS, LANES), force, other_force, start_modes.transpose(0, 1, 3, 2), faces * 2, block_count
    )
    back = lax.all_to_all(replies, ("face", "blk"), 0, 0, tiled=True)
    gram_rows, forces = outputs_call(back.reshape(BIN, 128), block_count)
    return gram_rows, forces.transpose(0, 3, 2, 1)


def shifted(x, axis, by):
    count = lax.axis_size(axis)
    return lax.ppermute(x, axis, [(i, (i + by) % count) for i in range(count)])


def gram_tiles(weighted, others):
    real_tile = jnp.einsum("kif,kjf->kij", weighted[0], others[0], precision=HIGH)
    real_tile = real_tile + jnp.einsum("kif,kjf->kij", weighted[1], others[1], precision=HIGH)
    imag_tile = jnp.einsum("kif,kjf->kij", weighted[0], others[1], precision=HIGH)
    imag_tile = imag_tile - jnp.einsum("kif,kjf->kij", weighted[1], others[0], precision=HIGH)
    return jnp.stack([real_tile, imag_tile])


def by_rows(record, face_area, face_tap, lever_table, start_modes):
    faces = record.shape[1]
    cycle = lax.axis_size("blk")
    block_count = BLK_DEV * cycle
    total_faces = faces * lax.axis_size("face")
    twiddle = jnp.asarray(band_twiddle())
    hops = record.reshape(BLK_DEV, HOP, faces)
    early = jnp.einsum("tk,btf->kbf", twiddle[:HOP], hops, precision=HIGH)
    late = jnp.einsum("tk,btf->kbf", twiddle[HOP:], hops, precision=HIGH)
    following = shifted(late[:, :1], "blk", -1)
    spectra = early + jnp.concatenate([late[:, 1:], following], axis=1)
    panels = jnp.stack([spectra[:BIN], spectra[BIN:]])
    weight = face_area.astype(jnp.float32) / 64.0
    gram_rows = gram_tiles(panels * weight, lax.all_gather(panels, "blk", axis=2, tiled=True))
    gram_rows = lax.psum(gram_rows, "face") / total_faces
    gram = lax.all_gather(gram_rows, "blk", axis=2, tiled=True)
    re, im = start_modes[0], start_modes[1]
    product = functools.partial(jnp.einsum, "kij,kjm->kim", precision=HIGH)
    for _ in range(PITERS):
        re, im = product(gram[0], re) - product(gram[1], im), product(gram[0], im) + product(gram[1], re)
        scale = jnp.sqrt(jnp.sum(re * re + im * im, axis=1, keepdims=True) / block_count + 1e-06)
        re, im = re / scale, im / scale
    own = BLK_DEV * lax.axis_index("blk")
    re = lax.dynamic_slice_in_dim(re, own, BLK_DEV, 1)
    im = lax.dynamic_slice_in_dim(im, own, BLK_DEV, 1)
    onehot = (face_tap[:, None] == jnp.arange(NTAP, dtype=jnp.int32)[None, :]).astype(jnp.float32)
    face_weight = weight[:, None] * jnp.dot(onehot, lever_table.astype(jnp.float32), precision=HIGH)
    load = jnp.einsum("pkbf,fc->pkbc", panels, face_weight, precision=HIGH) / math.sqrt(total_faces * block_count)
    force = functools.partial(jnp.einsum, "kbc,kbm->kmc", precision=HIGH)
    forces = jnp.stack([force(load[0], re) - force(load[1], im), force(load[0], im) + force(load[1], re)])
    return gram_rows, lax.psum(forces, ("blk", "face"))


def solution(mesh):
    fits = mesh.shape["blk"] * mesh.shape["face"] == BIN and mesh.shape["face"] == 2
    return jax.shard_map(
        by_bins if fits else by_rows,
        mesh=mesh,
        in_specs=(P("blk", ("grp", "face")), P("face"), P("face"), P(), P()),
        out_specs=(P(None, "grp", "blk", None), P(None, "grp", None, None)),
        check_vma=False,
    )
```

```python
import functools
import math

import jax
import jax.numpy as jnp
import ml_dtypes
import numpy as np
from jax import lax
from jax.experimental import pallas as pl
from jax.experimental.pallas import tpu as pltpu
from jax.sharding import PartitionSpec as P

NFFT = 1024
HOP = 512
BIN = 16
FIRST_BIN = 24
PITERS = 2
BLK_DEV = 2
NTAP = 512
NMODE = 4
NC = 3
LANES = 128
SPANS = 8
ROWS = 48
SPLIT = 2
F_LANE = 64
VMEM_LIMIT = 60 * 2**20

HIGH = lax.Precision.HIGHEST
NT = (((1,), (1,)), ((), ()))


def band_twiddle():
    steps = np.arange(NFFT)
    bins = FIRST_BIN + np.arange(BIN)
    angle = (steps[:, None] * bins[None, :] % NFFT) * (2.0 * math.pi / NFFT)
    window = 0.5 - 0.5 * np.cos(steps * (2.0 * math.pi / NFFT))
    scaling = np.sqrt(np.sum(window * window))
    cosine = window[:, None] * np.cos(angle) / scaling
    sine = -window[:, None] * np.sin(angle) / scaling
    return np.concatenate([cosine, sine], axis=1).astype(np.float32)


def thirds(x, cast):
    first = x.astype(jnp.bfloat16)
    rest = x - cast(first)
    second = rest.astype(jnp.bfloat16)
    third = (rest - cast(second)).astype(jnp.bfloat16)
    return first, second, third


def folded_twiddle():
    twiddle = band_twiddle().reshape(2, HOP, 2, BIN)
    rows = twiddle.transpose(0, 3, 2, 1).reshape(4 * BIN, HOP)
    first = rows.astype(ml_dtypes.bfloat16)
    rest = rows - first.astype(np.float32)
    second = rest.astype(ml_dtypes.bfloat16)
    third = (rest - second.astype(np.float32)).astype(ml_dtypes.bfloat16)
    return np.concatenate([first, second, third], axis=0)


def f32(x):
    return x.astype(jnp.float32)


def even_row(span):
    return 2 * span


def odd_row(span):
    return ROWS // 2 + 2 * span


def late_row(span):
    return 2 * SPANS + 2 * span if span < SPANS // 2 else ROWS // 2 + SPANS + 2 * span


def spectra_kernel(
    twiddle_hbm, record_hbm, area_hbm, tap_hbm, lever_hbm, out_ref, force_ref, twiddle, record, area, tap, lever, sems, record_sems
):
    faces = record.shape[1]
    width = faces // SPLIT
    small = [
        pltpu.make_async_copy(source, target, sems.at[i])
        for i, (source, target) in enumerate(((area_hbm, area), (tap_hbm, tap), (lever_hbm, lever), (twiddle_hbm, twiddle)))
    ]
    parts = [slice(q * width, (q + 1) * width) for q in range(SPLIT)]
    large = [
        pltpu.make_async_copy(record_hbm.at[:, part], record.at[:, part], record_sems.at[q]) for q, part in enumerate(parts)
    ]
    for copy in small[:3]:
        copy.start()
    small[3].start()
    for copy in large:
        copy.start()
    for copy in small[:3]:
        copy.wait()
    dot = functools.partial(jnp.dot, preferred_element_type=jnp.float32)
    root = jnp.sqrt(f32(area[...]) / 64.0)
    taps = lax.broadcasted_iota(jnp.int32, (NTAP, faces), 0)
    onehot = jnp.where(taps == tap[...], 1.0, 0.0).astype(jnp.bfloat16)
    force_ref[0:NC] = dot(f32(lever[...]).astype(jnp.bfloat16), onehot) * root
    force_ref[NC:] = jnp.zeros((8 - NC, faces), jnp.float32)
    small[3].wait()
    m = 4 * BIN
    for q, part in enumerate(parts):
        large[q].wait()
        halves = []
        for hop in range(BLK_DEV):
            first, second, third = thirds(record[hop * HOP : (hop + 1) * HOP, part], f32)
            one = dot(twiddle[...], first)
            two = dot(twiddle[: 2 * m], second)
            three = dot(twiddle[:m], third)
            halves.append((((one[2 * m :] + two[m:]) + three) + (one[m : 2 * m] + two[:m]) + one[:m]) * root[:, part])
        even = halves[0][: 2 * BIN] + halves[1][2 * BIN :]
        odd = halves[1][: 2 * BIN]
        late = halves[0][2 * BIN :]
        for k in range(BIN):
            pair = slice(2 * k, 2 * k + 2)
            for i in range(width // LANES):
                span, lane = q * (width // LANES) + i, slice(i * LANES, (i + 1) * LANES)
                out_ref[k, even_row(span) : even_row(span) + 2, :] = even[pair, lane]
                out_ref[k, odd_row(span) : odd_row(span) + 2, :] = odd[pair, lane]
                out_ref[k, late_row(span) : late_row(span) + 2, :] = late[pair, lane]


def spectra_call(twiddle, record, area, tap, lever):
    steps, faces = record.shape
    return pl.pallas_call(
        spectra_kernel,
        in_specs=[pl.BlockSpec(memory_space=pl.ANY)] * 5,
        out_specs=[pl.BlockSpec(memory_space=pltpu.VMEM)] * 2,
        out_shape=[
            jax.ShapeDtypeStruct((BIN, ROWS, LANES), jnp.float32),
            jax.ShapeDtypeStruct((8, faces), jnp.float32),
        ],
        scratch_shapes=[
            pltpu.VMEM(twiddle.shape, jnp.bfloat16),
            pltpu.VMEM(record.shape, jnp.float32),
            pltpu.VMEM((1, faces), jnp.int32),
            pltpu.VMEM((1, faces), jnp.int32),
            pltpu.VMEM(lever.shape, jnp.int32),
            pltpu.SemaphoreType.DMA((4,)),
            pltpu.SemaphoreType.DMA((SPLIT,)),
        ],
        compiler_params=pltpu.CompilerParams(vmem_limit_bytes=VMEM_LIMIT),
        name="band_spectra",
    )(twiddle, record, area, tap, lever)


def modes_kernel(total_faces, block_count, got_ref, force_ref, start_ref, out_ref):
    n = block_count
    dot = functools.partial(lax.dot_general, preferred_element_type=jnp.float32)
    is_odd = lax.broadcasted_iota(jnp.int32, (n, LANES), 0) % 2 == 1
    columns = []
    for face in range(2):
        base = face * (n // BLK_DEV) * ROWS
        for span in range(SPANS):
            rows = []
            for part in range(2):
                direct = got_ref[pl.ds(base + even_row(span) + part, n, stride=ROWS // 2), :]
                start = late_row(span) + part
                shift = 1 if start < ROWS // 2 else 2
                late = got_ref[pl.ds(base + start % (ROWS // 2), n, stride=ROWS // 2), :]
                rows.append(direct + jnp.where(is_odd, pltpu.roll(late, n - shift, 0), 0.0))
            columns.append(jnp.concatenate(rows, axis=0))
    q_all = jnp.concatenate(columns, axis=1)
    force = jnp.concatenate([force_ref[0], force_ref[1]], axis=1)
    m = 2 * n
    both = dot(jnp.concatenate([q_all, force], axis=0), q_all, NT, precision=HIGH)
    square, load = both[:m], both[m:]
    gram_re = (square[:n, :n] + square[n:, n:]) / total_faces
    gram_im = (square[:n, n:] - square[n:, :n]) / total_faces
    gram = jnp.concatenate(
        [jnp.concatenate([gram_re, -gram_im], axis=1), jnp.concatenate([gram_im, gram_re], axis=1)], axis=0
    )
    load = load / math.sqrt(total_faces * block_count)
    own = n // BLK_DEV * lax.axis_index("face") + lax.axis_index("blk")
    modes = jnp.concatenate([start_ref[0, own], start_ref[1, own]], axis=1)
    columns = [jnp.sum(gram * modes[i : i + 1], axis=1, keepdims=True) for i in range(NMODE)]
    columns = [y / jnp.sqrt(jnp.sum(y * y, axis=0, keepdims=True) / block_count + 1e-06) for y in columns]
    modes = jnp.concatenate([jnp.sum(gram * y, axis=0, keepdims=True) for y in columns], axis=0)
    modes = modes / jnp.sqrt(jnp.sum(modes * modes, axis=1, keepdims=True) / block_count + 1e-06)
    re, im = modes[:, :n], modes[:, n:]
    signed = jnp.concatenate([jnp.concatenate([re, -im], axis=1), jnp.concatenate([im, re], axis=1)], axis=0)
    lane = lax.broadcasted_iota(jnp.int32, (2 * NMODE, LANES), 1)
    line = lax.broadcasted_iota(jnp.int32, (2 * NMODE, LANES), 0)
    tail = jnp.zeros((2 * NMODE, LANES), jnp.float32)
    for c in range(NC):
        answer = jnp.sum(signed * load[c : c + 1], axis=1, keepdims=True)
        tail = jnp.where(lane == F_LANE + 2 * NMODE * c + line, answer, tail)
    tail = jnp.sum(tail, axis=0, keepdims=True)
    lower = jnp.concatenate([gram[n:], jnp.zeros((n, LANES - m), jnp.float32)], axis=1)
    moved = pltpu.roll(lower, m, 1)
    for d in range(n // BLK_DEV):
        reply = lower[2 * d : 2 * d + 1] + moved[2 * d + 1 : 2 * d + 2] + tail
        for face in range(2):
            out_ref[face * (n // BLK_DEV) + d] = reply


def modes_call(got, force, start, total_faces, block_count):
    vmem = pl.BlockSpec(memory_space=pltpu.VMEM)
    return pl.pallas_call(
        functools.partial(modes_kernel, total_faces, block_count),
        in_specs=[vmem, vmem, vmem],
        out_specs=vmem,
        out_shape=jax.ShapeDtypeStruct((BIN, 1, 128), jnp.float32),
        compiler_params=pltpu.CompilerParams(vmem_limit_bytes=32 * 2**20),
        name="bin_modes",
    )(got, force, start)


def outputs_kernel(block_count, back_ref, gram_ref, forces_ref):
    n = block_count
    back = back_ref[...]
    for part in range(2):
        for row in range(BLK_DEV):
            lane = 2 * n * row + n * (1 - part)
            gram_ref[part, :, row, :] = back[:, lane : lane + n]
    turned = back.T
    for part in range(2):
        for c in range(NC):
            line = F_LANE + 2 * NMODE * c + NMODE * part
            forces_ref[part, c] = turned[line : line + NMODE]


def outputs_call(back, block_count):
    vmem = pl.BlockSpec(memory_space=pltpu.VMEM)
    return pl.pallas_call(
        functools.partial(outputs_kernel, block_count),
        in_specs=[vmem],
        out_specs=[vmem, vmem],
        out_shape=[
            jax.ShapeDtypeStruct((2, BIN, BLK_DEV, block_count), jnp.float32),
            jax.ShapeDtypeStruct((2, NC, NMODE, BIN), jnp.float32),
        ],
        compiler_params=pltpu.CompilerParams(vmem_limit_bytes=16 * 2**20),
        name="outputs",
    )(back)


def by_bins(record, face_area, face_tap, lever_table, start_modes):
    faces = record.shape[1]
    cycle = lax.axis_size("blk")
    block_count = BLK_DEV * cycle
    messages, force = spectra_call(
        jnp.asarray(folded_twiddle()), record, face_area.reshape(1, faces), face_tap.reshape(1, faces), lever_table.T
    )
    forces = lax.all_gather(force, "face")
    got = lax.all_to_all(messages, ("face", "blk"), 0, 0, tiled=True)
    replies = modes_call(
        got.reshape(BIN * ROWS, LANES), forces, start_modes.transpose(0, 1, 3, 2), faces * 2, block_count
    )
    back = lax.all_to_all(replies, ("face", "blk"), 0, 0, tiled=True)
    gram_rows, forces = outputs_call(back.reshape(BIN, 128), block_count)
    return gram_rows, forces.transpose(0, 3, 2, 1)


def shifted(x, axis, by):
    count = lax.axis_size(axis)
    return lax.ppermute(x, axis, [(i, (i + by) % count) for i in range(count)])


def gram_tiles(weighted, others):
    real_tile = jnp.einsum("kif,kjf->kij", weighted[0], others[0], precision=HIGH)
    real_tile = real_tile + jnp.einsum("kif,kjf->kij", weighted[1], others[1], precision=HIGH)
    imag_tile = jnp.einsum("kif,kjf->kij", weighted[0], others[1], precision=HIGH)
    imag_tile = imag_tile - jnp.einsum("kif,kjf->kij", weighted[1], others[0], precision=HIGH)
    return jnp.stack([real_tile, imag_tile])


def by_rows(record, face_area, face_tap, lever_table, start_modes):
    faces = record.shape[1]
    cycle = lax.axis_size("blk")
    block_count = BLK_DEV * cycle
    total_faces = faces * lax.axis_size("face")
    twiddle = jnp.asarray(band_twiddle())
    hops = record.reshape(BLK_DEV, HOP, faces)
    early = jnp.einsum("tk,btf->kbf", twiddle[:HOP], hops, precision=HIGH)
    late = jnp.einsum("tk,btf->kbf", twiddle[HOP:], hops, precision=HIGH)
    following = shifted(late[:, :1], "blk", -1)
    spectra = early + jnp.concatenate([late[:, 1:], following], axis=1)
    panels = jnp.stack([spectra[:BIN], spectra[BIN:]])
    weight = face_area.astype(jnp.float32) / 64.0
    gram_rows = gram_tiles(panels * weight, lax.all_gather(panels, "blk", axis=2, tiled=True))
    gram_rows = lax.psum(gram_rows, "face") / total_faces
    gram = lax.all_gather(gram_rows, "blk", axis=2, tiled=True)
    re, im = start_modes[0], start_modes[1]
    product = functools.partial(jnp.einsum, "kij,kjm->kim", precision=HIGH)
    for _ in range(PITERS):
        re, im = product(gram[0], re) - product(gram[1], im), product(gram[0], im) + product(gram[1], re)
        scale = jnp.sqrt(jnp.sum(re * re + im * im, axis=1, keepdims=True) / block_count + 1e-06)
        re, im = re / scale, im / scale
    own = BLK_DEV * lax.axis_index("blk")
    re = lax.dynamic_slice_in_dim(re, own, BLK_DEV, 1)
    im = lax.dynamic_slice_in_dim(im, own, BLK_DEV, 1)
    onehot = (face_tap[:, None] == jnp.arange(NTAP, dtype=jnp.int32)[None, :]).astype(jnp.float32)
    face_weight = weight[:, None] * jnp.dot(onehot, lever_table.astype(jnp.float32), precision=HIGH)
    load = jnp.einsum("pkbf,fc->pkbc", panels, face_weight, precision=HIGH) / math.sqrt(total_faces * block_count)
    force = functools.partial(jnp.einsum, "kbc,kbm->kmc", precision=HIGH)
    forces = jnp.stack([force(load[0], re) - force(load[1], im), force(load[0], im) + force(load[1], re)])
    return gram_rows, lax.psum(forces, ("blk", "face"))


def solution(mesh):
    fits = mesh.shape["blk"] * mesh.shape["face"] == BIN and mesh.shape["face"] == 2
    return jax.shard_map(
        by_bins if fits else by_rows,
        mesh=mesh,
        in_specs=(P("blk", ("grp", "face")), P("face"), P("face"), P(), P()),
        out_specs=(P(None, "grp", "blk", None), P(None, "grp", None, None)),
        check_vma=False,
    )
```

```python
import functools
import math

import jax
import jax.numpy as jnp
import ml_dtypes
import numpy as np
from jax import lax
from jax.experimental import pallas as pl
from jax.experimental.pallas import tpu as pltpu
from jax.sharding import PartitionSpec as P

NFFT = 1024
HOP = 512
BIN = 16
FIRST_BIN = 24
PITERS = 2
BLK_DEV = 2
NTAP = 512
NMODE = 4
NC = 3
LANES = 128
SPANS = 8
ROWS = 48
SPLIT = 2
F_LANE = 64
VMEM_LIMIT = 60 * 2**20
OUT_TURN = 4
BACK_TURN = 4

HIGH = lax.Precision.HIGHEST
NT = (((1,), (1,)), ((), ()))


def band_twiddle():
    steps = np.arange(NFFT)
    bins = FIRST_BIN + np.arange(BIN)
    angle = (steps[:, None] * bins[None, :] % NFFT) * (2.0 * math.pi / NFFT)
    window = 0.5 - 0.5 * np.cos(steps * (2.0 * math.pi / NFFT))
    scaling = np.sqrt(np.sum(window * window))
    cosine = window[:, None] * np.cos(angle) / scaling
    sine = -window[:, None] * np.sin(angle) / scaling
    return np.concatenate([cosine, sine], axis=1).astype(np.float32)


def thirds(x, cast):
    first = x.astype(jnp.bfloat16)
    rest = x - cast(first)
    second = rest.astype(jnp.bfloat16)
    third = (rest - cast(second)).astype(jnp.bfloat16)
    return first, second, third


def folded_twiddle():
    twiddle = band_twiddle().reshape(2, HOP, 2, BIN)
    rows = twiddle.transpose(0, 3, 2, 1).reshape(4 * BIN, HOP)
    first = rows.astype(ml_dtypes.bfloat16)
    rest = rows - first.astype(np.float32)
    second = rest.astype(ml_dtypes.bfloat16)
    third = (rest - second.astype(np.float32)).astype(ml_dtypes.bfloat16)
    return np.concatenate([first, second, third], axis=0)


def turned(place, by):
    cycle = BIN // 2
    return place // cycle * cycle + (place + by) % cycle


def order(turn):
    return [[turned(place, turn) for place in range(BIN)]]


def f32(x):
    return x.astype(jnp.float32)


def even_row(span):
    return 2 * span


def odd_row(span):
    return ROWS // 2 + 2 * span


def late_row(span):
    return 2 * SPANS + 2 * span if span < SPANS // 2 else ROWS // 2 + SPANS + 2 * span


def spectra_kernel(twiddle_hbm, record_hbm, out_ref, twiddle, record, twiddle_sem, record_sems):
    faces = record.shape[1]
    width = faces // SPLIT
    parts = [slice(q * width, (q + 1) * width) for q in range(SPLIT)]
    small = pltpu.make_async_copy(twiddle_hbm.at[: twiddle.shape[0]], twiddle, twiddle_sem)
    large = [
        pltpu.make_async_copy(record_hbm.at[:, part], record.at[:, part], record_sems.at[q]) for q, part in enumerate(parts)
    ]
    small.start()
    for copy in large:
        copy.start()
    dot = functools.partial(jnp.dot, preferred_element_type=jnp.float32)
    small.wait()
    m = 4 * BIN
    for q, part in enumerate(parts):
        large[q].wait()
        halves = []
        for hop in range(BLK_DEV):
            first, second, third = thirds(record[hop * HOP : (hop + 1) * HOP, part], f32)
            one = dot(twiddle[...], first)
            two = dot(twiddle[: 2 * m], second)
            three = dot(twiddle[:m], third)
            halves.append(((one[2 * m :] + two[m:]) + three) + (one[m : 2 * m] + two[:m]) + one[:m])
        even = halves[0][: 2 * BIN] + halves[1][2 * BIN :]
        odd = halves[1][: 2 * BIN]
        late = halves[0][2 * BIN :]
        for k in range(BIN):
            pair = slice(2 * k, 2 * k + 2)
            slot = turned(k, BACK_TURN - OUT_TURN)
            for i in range(width // LANES):
                span, lane = q * (width // LANES) + i, slice(i * LANES, (i + 1) * LANES)
                out_ref[slot, even_row(span) : even_row(span) + 2, :] = even[pair, lane]
                out_ref[slot, odd_row(span) : odd_row(span) + 2, :] = odd[pair, lane]
                out_ref[slot, late_row(span) : late_row(span) + 2, :] = late[pair, lane]


def spectra_call(twiddle, record):
    steps, faces = record.shape
    return pl.pallas_call(
        spectra_kernel,
        in_specs=[pl.BlockSpec(memory_space=pl.ANY)] * 2,
        out_specs=pl.BlockSpec(memory_space=pltpu.VMEM),
        out_shape=jax.ShapeDtypeStruct((BIN, ROWS, LANES), jnp.float32),
        scratch_shapes=[
            pltpu.VMEM((12 * BIN, HOP), jnp.bfloat16),
            pltpu.VMEM(record.shape, jnp.float32),
            pltpu.SemaphoreType.DMA,
            pltpu.SemaphoreType.DMA((SPLIT,)),
        ],
        compiler_params=pltpu.CompilerParams(vmem_limit_bytes=VMEM_LIMIT),
        name="band_spectra",
    )(twiddle, record)


def force_kernel(area_ref, tap_ref, lever_ref, out_ref):
    faces = out_ref.shape[1]
    root = jnp.sqrt(f32(area_ref[...]) / 64.0)
    taps = lax.broadcasted_iota(jnp.int32, (NTAP, faces), 0)
    onehot = jnp.where(taps == tap_ref[...], 1.0, 0.0).astype(jnp.bfloat16)
    lever = f32(lever_ref[...]).astype(jnp.bfloat16)
    out_ref[0:NC] = jnp.dot(lever, onehot, preferred_element_type=jnp.float32) * root
    out_ref[NC : NC + 1] = root
    out_ref[NC + 1 :] = jnp.zeros((7 - NC, faces), jnp.float32)


def force_call(area, tap, lever):
    vmem = pl.BlockSpec(memory_space=pltpu.VMEM)
    return pl.pallas_call(
        force_kernel,
        in_specs=[vmem, vmem, vmem],
        out_specs=vmem,
        out_shape=jax.ShapeDtypeStruct((8, area.shape[1]), jnp.float32),
        cost_estimate=pl.CostEstimate(flops=2**21, bytes_accessed=2**16, transcendentals=0),
        name="force_rows",
    )(area, tap, lever)


def modes_kernel(total_faces, block_count, got_ref, force_ref, start_ref, out_ref):
    n = block_count
    dot = functools.partial(lax.dot_general, preferred_element_type=jnp.float32)
    is_odd = lax.broadcasted_iota(jnp.int32, (n, LANES), 0) % 2 == 1
    columns = []
    for face in range(2):
        base = face * (n // BLK_DEV) * ROWS
        for span in range(SPANS):
            rows = []
            for part in range(2):
                direct = got_ref[pl.ds(base + even_row(span) + part, n, stride=ROWS // 2), :]
                start = late_row(span) + part
                shift = 1 if start < ROWS // 2 else 2
                late = got_ref[pl.ds(base + start % (ROWS // 2), n, stride=ROWS // 2), :]
                rows.append(pltpu.roll(direct + jnp.where(is_odd, pltpu.roll(late, n - shift, 0), 0.0), BLK_DEV * OUT_TURN, 0))
            columns.append(jnp.concatenate(rows, axis=0))
    force = jnp.concatenate([force_ref[0], force_ref[1]], axis=1)
    q_all = jnp.concatenate(columns, axis=1) * force[NC : NC + 1]
    m = 2 * n
    both = dot(jnp.concatenate([q_all, force], axis=0), q_all, NT, precision=HIGH)
    square, load = both[:m], both[m:]
    gram_re = (square[:n, :n] + square[n:, n:]) / total_faces
    gram_im = (square[:n, n:] - square[n:, :n]) / total_faces
    gram = jnp.concatenate(
        [jnp.concatenate([gram_re, -gram_im], axis=1), jnp.concatenate([gram_im, gram_re], axis=1)], axis=0
    )
    load = load / math.sqrt(total_faces * block_count)
    cycle = n // BLK_DEV
    own = cycle * lax.axis_index("face") + lax.rem(lax.axis_index("blk") + (cycle - BACK_TURN), cycle)
    modes = jnp.concatenate([start_ref[0, own], start_ref[1, own]], axis=1)
    columns = [jnp.sum(gram * modes[i : i + 1], axis=1, keepdims=True) for i in range(NMODE)]
    columns = [y / jnp.sqrt(jnp.sum(y * y, axis=0, keepdims=True) / block_count + 1e-06) for y in columns]
    modes = jnp.concatenate([jnp.sum(gram * y, axis=0, keepdims=True) for y in columns], axis=0)
    modes = modes / jnp.sqrt(jnp.sum(modes * modes, axis=1, keepdims=True) / block_count + 1e-06)
    re, im = modes[:, :n], modes[:, n:]
    signed = jnp.concatenate([jnp.concatenate([re, -im], axis=1), jnp.concatenate([im, re], axis=1)], axis=0)
    lane = lax.broadcasted_iota(jnp.int32, (2 * NMODE, LANES), 1)
    line = lax.broadcasted_iota(jnp.int32, (2 * NMODE, LANES), 0)
    tail = jnp.zeros((2 * NMODE, LANES), jnp.float32)
    for c in range(NC):
        answer = jnp.sum(signed * load[c : c + 1], axis=1, keepdims=True)
        tail = jnp.where(lane == F_LANE + 2 * NMODE * c + line, answer, tail)
    tail = jnp.sum(tail, axis=0, keepdims=True)
    lower = jnp.concatenate([gram[n:], jnp.zeros((n, LANES - m), jnp.float32)], axis=1)
    moved = pltpu.roll(lower, m, 1)
    for d in range(cycle):
        reply = lower[2 * d : 2 * d + 1] + moved[2 * d + 1 : 2 * d + 2] + tail
        for face in range(2):
            out_ref[turned(face * cycle + d, -BACK_TURN)] = reply


def modes_call(got, force, start, total_faces, block_count):
    vmem = pl.BlockSpec(memory_space=pltpu.VMEM)
    return pl.pallas_call(
        functools.partial(modes_kernel, total_faces, block_count),
        in_specs=[vmem, vmem, vmem],
        out_specs=vmem,
        out_shape=jax.ShapeDtypeStruct((BIN, 1, 128), jnp.float32),
        compiler_params=pltpu.CompilerParams(vmem_limit_bytes=32 * 2**20),
        name="bin_modes",
    )(got, force, start)


def outputs_kernel(block_count, back_ref, gram_ref, forces_ref):
    n = block_count
    back = back_ref[...]
    for part in range(2):
        for row in range(BLK_DEV):
            lane = 2 * n * row + n * (1 - part)
            gram_ref[part, :, row, :] = back[:, lane : lane + n]
    turned = back.T
    for part in range(2):
        for c in range(NC):
            line = F_LANE + 2 * NMODE * c + NMODE * part
            forces_ref[part, c] = turned[line : line + NMODE]


def outputs_call(back, block_count):
    vmem = pl.BlockSpec(memory_space=pltpu.VMEM)
    return pl.pallas_call(
        functools.partial(outputs_kernel, block_count),
        in_specs=[vmem],
        out_specs=[vmem, vmem],
        out_shape=[
            jax.ShapeDtypeStruct((2, BIN, BLK_DEV, block_count), jnp.float32),
            jax.ShapeDtypeStruct((2, NC, NMODE, BIN), jnp.float32),
        ],
        compiler_params=pltpu.CompilerParams(vmem_limit_bytes=16 * 2**20),
        name="outputs",
    )(back)


def by_bins(record, face_area, face_tap, lever_table, start_modes):
    faces = record.shape[1]
    cycle = lax.axis_size("blk")
    block_count = BLK_DEV * cycle
    messages = spectra_call(jnp.asarray(folded_twiddle()), record)
    force = force_call(face_area.reshape(1, faces), face_tap.reshape(1, faces), lever_table.T)
    forces = lax.all_gather(force, "face")
    got = lax.all_to_all(messages, ("face", "blk"), 0, 0, tiled=True, axis_index_groups=order(OUT_TURN))
    replies = modes_call(
        got.reshape(BIN * ROWS, LANES), forces, start_modes.transpose(0, 1, 3, 2), faces * 2, block_count
    )
    back = lax.all_to_all(replies, ("face", "blk"), 0, 0, tiled=True, axis_index_groups=order(BACK_TURN))
    gram_rows, forces = outputs_call(back.reshape(BIN, 128), block_count)
    return gram_rows, forces.transpose(0, 3, 2, 1)


def shifted(x, axis, by):
    count = lax.axis_size(axis)
    return lax.ppermute(x, axis, [(i, (i + by) % count) for i in range(count)])


def gram_tiles(weighted, others):
    real_tile = jnp.einsum("kif,kjf->kij", weighted[0], others[0], precision=HIGH)
    real_tile = real_tile + jnp.einsum("kif,kjf->kij", weighted[1], others[1], precision=HIGH)
    imag_tile = jnp.einsum("kif,kjf->kij", weighted[0], others[1], precision=HIGH)
    imag_tile = imag_tile - jnp.einsum("kif,kjf->kij", weighted[1], others[0], precision=HIGH)
    return jnp.stack([real_tile, imag_tile])


def by_rows(record, face_area, face_tap, lever_table, start_modes):
    faces = record.shape[1]
    cycle = lax.axis_size("blk")
    block_count = BLK_DEV * cycle
    total_faces = faces * lax.axis_size("face")
    twiddle = jnp.asarray(band_twiddle())
    hops = record.reshape(BLK_DEV, HOP, faces)
    early = jnp.einsum("tk,btf->kbf", twiddle[:HOP], hops, precision=HIGH)
    late = jnp.einsum("tk,btf->kbf", twiddle[HOP:], hops, precision=HIGH)
    following = shifted(late[:, :1], "blk", -1)
    spectra = early + jnp.concatenate([late[:, 1:], following], axis=1)
    panels = jnp.stack([spectra[:BIN], spectra[BIN:]])
    weight = face_area.astype(jnp.float32) / 64.0
    gram_rows = gram_tiles(panels * weight, lax.all_gather(panels, "blk", axis=2, tiled=True))
    gram_rows = lax.psum(gram_rows, "face") / total_faces
    gram = lax.all_gather(gram_rows, "blk", axis=2, tiled=True)
    re, im = start_modes[0], start_modes[1]
    product = functools.partial(jnp.einsum, "kij,kjm->kim", precision=HIGH)
    for _ in range(PITERS):
        re, im = product(gram[0], re) - product(gram[1], im), product(gram[0], im) + product(gram[1], re)
        scale = jnp.sqrt(jnp.sum(re * re + im * im, axis=1, keepdims=True) / block_count + 1e-06)
        re, im = re / scale, im / scale
    own = BLK_DEV * lax.axis_index("blk")
    re = lax.dynamic_slice_in_dim(re, own, BLK_DEV, 1)
    im = lax.dynamic_slice_in_dim(im, own, BLK_DEV, 1)
    onehot = (face_tap[:, None] == jnp.arange(NTAP, dtype=jnp.int32)[None, :]).astype(jnp.float32)
    face_weight = weight[:, None] * jnp.dot(onehot, lever_table.astype(jnp.float32), precision=HIGH)
    load = jnp.einsum("pkbf,fc->pkbc", panels, face_weight, precision=HIGH) / math.sqrt(total_faces * block_count)
    force = functools.partial(jnp.einsum, "kbc,kbm->kmc", precision=HIGH)
    forces = jnp.stack([force(load[0], re) - force(load[1], im), force(load[0], im) + force(load[1], re)])
    return gram_rows, lax.psum(forces, ("blk", "face"))


def solution(mesh):
    fits = mesh.shape["blk"] * mesh.shape["face"] == BIN and mesh.shape["face"] == 2
    return jax.shard_map(
        by_bins if fits else by_rows,
        mesh=mesh,
        in_specs=(P("blk", ("grp", "face")), P("face"), P("face"), P(), P()),
        out_specs=(P(None, "grp", "blk", None), P(None, "grp", None, None)),
        check_vma=False,
    )
```

```python
import functools
import math

import jax
import jax.numpy as jnp
import ml_dtypes
import numpy as np
from jax import lax
from jax.experimental import pallas as pl
from jax.experimental.pallas import tpu as pltpu
from jax.sharding import PartitionSpec as P

NFFT = 1024
HOP = 512
BIN = 16
FIRST_BIN = 24
PITERS = 2
BLK_DEV = 2
NTAP = 512
NMODE = 4
NC = 3
LANES = 128
SPANS = 8
ROWS = 48
SPLIT = 2
F_LANE = 64
VMEM_LIMIT = 60 * 2**20
TURN = 5
FIRST_FACE = 1

HIGH = lax.Precision.HIGHEST
NT = (((1,), (1,)), ((), ()))


def band_twiddle():
    steps = np.arange(NFFT)
    bins = FIRST_BIN + np.arange(BIN)
    angle = (steps[:, None] * bins[None, :] % NFFT) * (2.0 * math.pi / NFFT)
    window = 0.5 - 0.5 * np.cos(steps * (2.0 * math.pi / NFFT))
    scaling = np.sqrt(np.sum(window * window))
    cosine = window[:, None] * np.cos(angle) / scaling
    sine = -window[:, None] * np.sin(angle) / scaling
    return np.concatenate([cosine, sine], axis=1).astype(np.float32)


def thirds(x, cast):
    first = x.astype(jnp.bfloat16)
    rest = x - cast(first)
    second = rest.astype(jnp.bfloat16)
    third = (rest - cast(second)).astype(jnp.bfloat16)
    return first, second, third


def folded_twiddle():
    twiddle = band_twiddle().reshape(2, HOP, 2, BIN)
    rows = twiddle.transpose(0, 3, 2, 1).reshape(4 * BIN, HOP)
    first = rows.astype(ml_dtypes.bfloat16)
    rest = rows - first.astype(np.float32)
    second = rest.astype(ml_dtypes.bfloat16)
    third = (rest - second.astype(np.float32)).astype(ml_dtypes.bfloat16)
    return np.concatenate([first, second, third], axis=0)


def turned(place, by):
    cycle = BIN // 2
    return place // cycle * cycle + (place + by) % cycle


def order(turn):
    return [[(turned(place, turn) + FIRST_FACE * (BIN // 2)) % BIN for place in range(BIN)]]


def f32(x):
    return x.astype(jnp.float32)


def even_row(span):
    return 2 * span


def odd_row(span):
    return ROWS // 2 + 2 * span


def late_row(span):
    return 2 * SPANS + 2 * span if span < SPANS // 2 else ROWS // 2 + SPANS + 2 * span


def spectra_kernel(twiddle_hbm, record_hbm, out_ref, twiddle, record, twiddle_sem, record_sems):
    faces = record.shape[1]
    width = faces // SPLIT
    parts = [slice(q * width, (q + 1) * width) for q in range(SPLIT)]
    small = pltpu.make_async_copy(twiddle_hbm.at[: twiddle.shape[0]], twiddle, twiddle_sem)
    large = [
        pltpu.make_async_copy(record_hbm.at[:, part], record.at[:, part], record_sems.at[q]) for q, part in enumerate(parts)
    ]
    small.start()
    for copy in large:
        copy.start()
    dot = functools.partial(jnp.dot, preferred_element_type=jnp.float32)
    small.wait()
    m = 4 * BIN
    for q, part in enumerate(parts):
        large[q].wait()
        halves = []
        for hop in range(BLK_DEV):
            first, second, third = thirds(record[hop * HOP : (hop + 1) * HOP, part], f32)
            one = dot(twiddle[...], first)
            two = dot(twiddle[: 2 * m], second)
            three = dot(twiddle[:m], third)
            halves.append(((one[2 * m :] + two[m:]) + three) + (one[m : 2 * m] + two[:m]) + one[:m])
        even = halves[0][: 2 * BIN] + halves[1][2 * BIN :]
        odd = halves[1][: 2 * BIN]
        late = halves[0][2 * BIN :]
        for k in range(BIN):
            pair = slice(2 * k, 2 * k + 2)
            for i in range(width // LANES):
                span, lane = q * (width // LANES) + i, slice(i * LANES, (i + 1) * LANES)
                out_ref[k, even_row(span) : even_row(span) + 2, :] = even[pair, lane]
                out_ref[k, odd_row(span) : odd_row(span) + 2, :] = odd[pair, lane]
                out_ref[k, late_row(span) : late_row(span) + 2, :] = late[pair, lane]


def spectra_call(twiddle, record):
    steps, faces = record.shape
    return pl.pallas_call(
        spectra_kernel,
        in_specs=[pl.BlockSpec(memory_space=pl.ANY)] * 2,
        out_specs=pl.BlockSpec(memory_space=pltpu.VMEM),
        out_shape=jax.ShapeDtypeStruct((BIN, ROWS, LANES), jnp.float32),
        scratch_shapes=[
            pltpu.VMEM((12 * BIN, HOP), jnp.bfloat16),
            pltpu.VMEM(record.shape, jnp.float32),
            pltpu.SemaphoreType.DMA,
            pltpu.SemaphoreType.DMA((SPLIT,)),
        ],
        compiler_params=pltpu.CompilerParams(vmem_limit_bytes=VMEM_LIMIT),
        name="band_spectra",
    )(twiddle, record)


def force_kernel(area_ref, tap_ref, lever_ref, out_ref):
    faces = out_ref.shape[1]
    root = jnp.sqrt(f32(area_ref[...]) / 64.0)
    taps = lax.broadcasted_iota(jnp.int32, (NTAP, faces), 0)
    onehot = jnp.where(taps == tap_ref[...], 1.0, 0.0).astype(jnp.bfloat16)
    lever = f32(lever_ref[...]).astype(jnp.bfloat16)
    out_ref[0:NC] = jnp.dot(lever, onehot, preferred_element_type=jnp.float32) * root
    out_ref[NC : NC + 1] = root
    out_ref[NC + 1 :] = jnp.zeros((7 - NC, faces), jnp.float32)


def force_call(area, tap, lever):
    vmem = pl.BlockSpec(memory_space=pltpu.VMEM)
    return pl.pallas_call(
        force_kernel,
        in_specs=[vmem, vmem, vmem],
        out_specs=vmem,
        out_shape=jax.ShapeDtypeStruct((8, area.shape[1]), jnp.float32),
        cost_estimate=pl.CostEstimate(flops=2**21, bytes_accessed=2**16, transcendentals=0),
        name="force_rows",
    )(area, tap, lever)


def modes_kernel(total_faces, block_count, got_ref, force_ref, start_ref, out_ref):
    n = block_count
    dot = functools.partial(lax.dot_general, preferred_element_type=jnp.float32)
    is_odd = lax.broadcasted_iota(jnp.int32, (n, LANES), 0) % 2 == 1
    columns = []
    for face in range(2):
        base = face * (n // BLK_DEV) * ROWS
        for span in range(SPANS):
            rows = []
            for part in range(2):
                direct = got_ref[pl.ds(base + even_row(span) + part, n, stride=ROWS // 2), :]
                start = late_row(span) + part
                shift = 1 if start < ROWS // 2 else 2
                late = got_ref[pl.ds(base + start % (ROWS // 2), n, stride=ROWS // 2), :]
                rows.append(pltpu.roll(direct + jnp.where(is_odd, pltpu.roll(late, n - shift, 0), 0.0), BLK_DEV * TURN, 0))
            columns.append(jnp.concatenate(rows, axis=0))
    force = jnp.concatenate([force_ref[FIRST_FACE], force_ref[1 - FIRST_FACE]], axis=1)
    q_all = jnp.concatenate(columns, axis=1) * force[NC : NC + 1]
    m = 2 * n
    both = dot(jnp.concatenate([q_all, force], axis=0), q_all, NT, precision=HIGH)
    square, load = both[:m], both[m:]
    gram_re = (square[:n, :n] + square[n:, n:]) / total_faces
    gram_im = (square[:n, n:] - square[n:, :n]) / total_faces
    gram = jnp.concatenate(
        [jnp.concatenate([gram_re, -gram_im], axis=1), jnp.concatenate([gram_im, gram_re], axis=1)], axis=0
    )
    load = load / math.sqrt(total_faces * block_count)
    cycle = n // BLK_DEV
    own = cycle * lax.rem(lax.axis_index("face") + FIRST_FACE, 2) + lax.rem(lax.axis_index("blk") + (cycle - TURN), cycle)
    modes = jnp.concatenate([start_ref[0, own], start_ref[1, own]], axis=1)
    columns = [jnp.sum(gram * modes[i : i + 1], axis=1, keepdims=True) for i in range(NMODE)]
    columns = [y / jnp.sqrt(jnp.sum(y * y, axis=0, keepdims=True) / block_count + 1e-06) for y in columns]
    modes = jnp.concatenate([jnp.sum(gram * y, axis=0, keepdims=True) for y in columns], axis=0)
    modes = modes / jnp.sqrt(jnp.sum(modes * modes, axis=1, keepdims=True) / block_count + 1e-06)
    re, im = modes[:, :n], modes[:, n:]
    signed = jnp.concatenate([jnp.concatenate([re, -im], axis=1), jnp.concatenate([im, re], axis=1)], axis=0)
    lane = lax.broadcasted_iota(jnp.int32, (2 * NMODE, LANES), 1)
    line = lax.broadcasted_iota(jnp.int32, (2 * NMODE, LANES), 0)
    tail = jnp.zeros((2 * NMODE, LANES), jnp.float32)
    for c in range(NC):
        answer = jnp.sum(signed * load[c : c + 1], axis=1, keepdims=True)
        tail = jnp.where(lane == F_LANE + 2 * NMODE * c + line, answer, tail)
    tail = jnp.sum(tail, axis=0, keepdims=True)
    lower = jnp.concatenate([gram[n:], jnp.zeros((n, LANES - m), jnp.float32)], axis=1)
    moved = pltpu.roll(lower, m, 1)
    for d in range(cycle):
        reply = lower[2 * d : 2 * d + 1] + moved[2 * d + 1 : 2 * d + 2] + tail
        for face in range(2):
            out_ref[turned(face * cycle + d, -TURN)] = reply


def modes_call(got, force, start, total_faces, block_count):
    vmem = pl.BlockSpec(memory_space=pltpu.VMEM)
    return pl.pallas_call(
        functools.partial(modes_kernel, total_faces, block_count),
        in_specs=[vmem, vmem, vmem],
        out_specs=vmem,
        out_shape=jax.ShapeDtypeStruct((BIN, 1, 128), jnp.float32),
        compiler_params=pltpu.CompilerParams(vmem_limit_bytes=32 * 2**20),
        name="bin_modes",
    )(got, force, start)


def outputs_kernel(block_count, back_ref, gram_ref, forces_ref):
    n = block_count
    back = back_ref[...]
    for part in range(2):
        for row in range(BLK_DEV):
            lane = 2 * n * row + n * (1 - part)
            gram_ref[part, :, row, :] = back[:, lane : lane + n]
    turned = back.T
    for part in range(2):
        for c in range(NC):
            line = F_LANE + 2 * NMODE * c + NMODE * part
            forces_ref[part, c] = turned[line : line + NMODE]


def outputs_call(back, block_count):
    vmem = pl.BlockSpec(memory_space=pltpu.VMEM)
    return pl.pallas_call(
        functools.partial(outputs_kernel, block_count),
        in_specs=[vmem],
        out_specs=[vmem, vmem],
        out_shape=[
            jax.ShapeDtypeStruct((2, BIN, BLK_DEV, block_count), jnp.float32),
            jax.ShapeDtypeStruct((2, NC, NMODE, BIN), jnp.float32),
        ],
        compiler_params=pltpu.CompilerParams(vmem_limit_bytes=16 * 2**20),
        name="outputs",
    )(back)


def by_bins(record, face_area, face_tap, lever_table, start_modes):
    faces = record.shape[1]
    cycle = lax.axis_size("blk")
    block_count = BLK_DEV * cycle
    messages = spectra_call(jnp.asarray(folded_twiddle()), record)
    force = force_call(face_area.reshape(1, faces), face_tap.reshape(1, faces), lever_table.T)
    forces = lax.all_gather(force, "face")
    got = lax.all_to_all(messages, ("face", "blk"), 0, 0, tiled=True, axis_index_groups=order(TURN))
    replies = modes_call(
        got.reshape(BIN * ROWS, LANES), forces, start_modes.transpose(0, 1, 3, 2), faces * 2, block_count
    )
    back = lax.all_to_all(replies, ("face", "blk"), 0, 0, tiled=True, axis_index_groups=order(TURN))
    gram_rows, forces = outputs_call(back.reshape(BIN, 128), block_count)
    return gram_rows, forces.transpose(0, 3, 2, 1)


def shifted(x, axis, by):
    count = lax.axis_size(axis)
    return lax.ppermute(x, axis, [(i, (i + by) % count) for i in range(count)])


def gram_tiles(weighted, others):
    real_tile = jnp.einsum("kif,kjf->kij", weighted[0], others[0], precision=HIGH)
    real_tile = real_tile + jnp.einsum("kif,kjf->kij", weighted[1], others[1], precision=HIGH)
    imag_tile = jnp.einsum("kif,kjf->kij", weighted[0], others[1], precision=HIGH)
    imag_tile = imag_tile - jnp.einsum("kif,kjf->kij", weighted[1], others[0], precision=HIGH)
    return jnp.stack([real_tile, imag_tile])


def by_rows(record, face_area, face_tap, lever_table, start_modes):
    faces = record.shape[1]
    cycle = lax.axis_size("blk")
    block_count = BLK_DEV * cycle
    total_faces = faces * lax.axis_size("face")
    twiddle = jnp.asarray(band_twiddle())
    hops = record.reshape(BLK_DEV, HOP, faces)
    early = jnp.einsum("tk,btf->kbf", twiddle[:HOP], hops, precision=HIGH)
    late = jnp.einsum("tk,btf->kbf", twiddle[HOP:], hops, precision=HIGH)
    following = shifted(late[:, :1], "blk", -1)
    spectra = early + jnp.concatenate([late[:, 1:], following], axis=1)
    panels = jnp.stack([spectra[:BIN], spectra[BIN:]])
    weight = face_area.astype(jnp.float32) / 64.0
    gram_rows = gram_tiles(panels * weight, lax.all_gather(panels, "blk", axis=2, tiled=True))
    gram_rows = lax.psum(gram_rows, "face") / total_faces
    gram = lax.all_gather(gram_rows, "blk", axis=2, tiled=True)
    re, im = start_modes[0], start_modes[1]
    product = functools.partial(jnp.einsum, "kij,kjm->kim", precision=HIGH)
    for _ in range(PITERS):
        re, im = product(gram[0], re) - product(gram[1], im), product(gram[0], im) + product(gram[1], re)
        scale = jnp.sqrt(jnp.sum(re * re + im * im, axis=1, keepdims=True) / block_count + 1e-06)
        re, im = re / scale, im / scale
    own = BLK_DEV * lax.axis_index("blk")
    re = lax.dynamic_slice_in_dim(re, own, BLK_DEV, 1)
    im = lax.dynamic_slice_in_dim(im, own, BLK_DEV, 1)
    onehot = (face_tap[:, None] == jnp.arange(NTAP, dtype=jnp.int32)[None, :]).astype(jnp.float32)
    face_weight = weight[:, None] * jnp.dot(onehot, lever_table.astype(jnp.float32), precision=HIGH)
    load = jnp.einsum("pkbf,fc->pkbc", panels, face_weight, precision=HIGH) / math.sqrt(total_faces * block_count)
    force = functools.partial(jnp.einsum, "kbc,kbm->kmc", precision=HIGH)
    forces = jnp.stack([force(load[0], re) - force(load[1], im), force(load[0], im) + force(load[1], re)])
    return gram_rows, lax.psum(forces, ("blk", "face"))


def solution(mesh):
    fits = mesh.shape["blk"] * mesh.shape["face"] == BIN and mesh.shape["face"] == 2
    return jax.shard_map(
        by_bins if fits else by_rows,
        mesh=mesh,
        in_specs=(P("blk", ("grp", "face")), P("face"), P("face"), P(), P()),
        out_specs=(P(None, "grp", "blk", None), P(None, "grp", None, None)),
        check_vma=False,
    )
```

```python
import functools
import math

import jax
import jax.numpy as jnp
import ml_dtypes
import numpy as np
from jax import lax
from jax.experimental import pallas as pl
from jax.experimental.pallas import tpu as pltpu
from jax.sharding import PartitionSpec as P

NFFT = 1024
HOP = 512
BIN = 16
FIRST_BIN = 24
PITERS = 2
BLK_DEV = 2
NTAP = 512
NMODE = 4
NC = 3
LANES = 128
SPANS = 8
ROWS = 48
SPLIT = 2
F_LANE = 64
VMEM_LIMIT = 60 * 2**20
TURN = 5
FIRST_FACE = 1
TURNS = (5, 1)

HIGH = lax.Precision.HIGHEST
NT = (((1,), (1,)), ((), ()))


def band_twiddle():
    steps = np.arange(NFFT)
    bins = FIRST_BIN + np.arange(BIN)
    angle = (steps[:, None] * bins[None, :] % NFFT) * (2.0 * math.pi / NFFT)
    window = 0.5 - 0.5 * np.cos(steps * (2.0 * math.pi / NFFT))
    scaling = np.sqrt(np.sum(window * window))
    cosine = window[:, None] * np.cos(angle) / scaling
    sine = -window[:, None] * np.sin(angle) / scaling
    return np.concatenate([cosine, sine], axis=1).astype(np.float32)


def thirds(x, cast):
    first = x.astype(jnp.bfloat16)
    rest = x - cast(first)
    second = rest.astype(jnp.bfloat16)
    third = (rest - cast(second)).astype(jnp.bfloat16)
    return first, second, third


def folded_twiddle():
    twiddle = band_twiddle().reshape(2, HOP, 2, BIN)
    rows = twiddle.transpose(0, 3, 2, 1).reshape(4 * BIN, HOP)
    first = rows.astype(ml_dtypes.bfloat16)
    rest = rows - first.astype(np.float32)
    second = rest.astype(ml_dtypes.bfloat16)
    third = (rest - second.astype(np.float32)).astype(ml_dtypes.bfloat16)
    return np.concatenate([first, second, third], axis=0)


def turned(place, by):
    cycle = BIN // 2
    return place // cycle * cycle + (place + by) % cycle


def order(turn):
    return [[(turned(place, turn) + FIRST_FACE * (BIN // 2)) % BIN for place in range(BIN)]]


def spectra_order():
    cycle = BIN // 2
    faces = (FIRST_FACE, 1 - FIRST_FACE)
    return [[faces[half] * cycle + (place + TURNS[half]) % cycle for half in range(2) for place in range(cycle)]]


def f32(x):
    return x.astype(jnp.float32)


def even_row(span):
    return 2 * span


def odd_row(span):
    return ROWS // 2 + 2 * span


def late_row(span):
    return 2 * SPANS + 2 * span if span < SPANS // 2 else ROWS // 2 + SPANS + 2 * span


def spectra_kernel(twiddle_hbm, record_hbm, out_ref, twiddle, record, twiddle_sem, record_sems):
    faces = record.shape[1]
    width = faces // SPLIT
    parts = [slice(q * width, (q + 1) * width) for q in range(SPLIT)]
    small = pltpu.make_async_copy(twiddle_hbm.at[: twiddle.shape[0]], twiddle, twiddle_sem)
    large = [
        pltpu.make_async_copy(record_hbm.at[:, part], record.at[:, part], record_sems.at[q]) for q, part in enumerate(parts)
    ]
    small.start()
    for copy in large:
        copy.start()
    dot = functools.partial(jnp.dot, preferred_element_type=jnp.float32)
    small.wait()
    m = 4 * BIN
    for q, part in enumerate(parts):
        large[q].wait()
        halves = []
        for hop in range(BLK_DEV):
            first, second, third = thirds(record[hop * HOP : (hop + 1) * HOP, part], f32)
            one = dot(twiddle[...], first)
            two = dot(twiddle[: 2 * m], second)
            three = dot(twiddle[:m], third)
            halves.append(((one[2 * m :] + two[m:]) + three) + (one[m : 2 * m] + two[:m]) + one[:m])
        even = halves[0][: 2 * BIN] + halves[1][2 * BIN :]
        odd = halves[1][: 2 * BIN]
        late = halves[0][2 * BIN :]
        for k in range(BIN):
            pair = slice(2 * k, 2 * k + 2)
            slot = turned(k, TURN - TURNS[k // (BIN // 2)])
            for i in range(width // LANES):
                span, lane = q * (width // LANES) + i, slice(i * LANES, (i + 1) * LANES)
                out_ref[slot, even_row(span) : even_row(span) + 2, :] = even[pair, lane]
                out_ref[slot, odd_row(span) : odd_row(span) + 2, :] = odd[pair, lane]
                out_ref[slot, late_row(span) : late_row(span) + 2, :] = late[pair, lane]


def spectra_call(twiddle, record):
    steps, faces = record.shape
    return pl.pallas_call(
        spectra_kernel,
        in_specs=[pl.BlockSpec(memory_space=pl.ANY)] * 2,
        out_specs=pl.BlockSpec(memory_space=pltpu.VMEM),
        out_shape=jax.ShapeDtypeStruct((BIN, ROWS, LANES), jnp.float32),
        scratch_shapes=[
            pltpu.VMEM((12 * BIN, HOP), jnp.bfloat16),
            pltpu.VMEM(record.shape, jnp.float32),
            pltpu.SemaphoreType.DMA,
            pltpu.SemaphoreType.DMA((SPLIT,)),
        ],
        compiler_params=pltpu.CompilerParams(vmem_limit_bytes=VMEM_LIMIT),
        name="band_spectra",
    )(twiddle, record)


def force_kernel(area_ref, tap_ref, lever_ref, out_ref):
    faces = out_ref.shape[1]
    root = jnp.sqrt(f32(area_ref[...]) / 64.0)
    taps = lax.broadcasted_iota(jnp.int32, (NTAP, faces), 0)
    onehot = jnp.where(taps == tap_ref[...], 1.0, 0.0).astype(jnp.bfloat16)
    lever = f32(lever_ref[...]).astype(jnp.bfloat16)
    out_ref[0:NC] = jnp.dot(lever, onehot, preferred_element_type=jnp.float32) * root
    out_ref[NC : NC + 1] = root
    out_ref[NC + 1 :] = jnp.zeros((7 - NC, faces), jnp.float32)


def force_call(area, tap, lever):
    vmem = pl.BlockSpec(memory_space=pltpu.VMEM)
    return pl.pallas_call(
        force_kernel,
        in_specs=[vmem, vmem, vmem],
        out_specs=vmem,
        out_shape=jax.ShapeDtypeStruct((8, area.shape[1]), jnp.float32),
        cost_estimate=pl.CostEstimate(flops=2**21, bytes_accessed=2**16, transcendentals=0),
        name="force_rows",
    )(area, tap, lever)


def modes_kernel(total_faces, block_count, got_ref, force_ref, start_ref, out_ref):
    n = block_count
    dot = functools.partial(lax.dot_general, preferred_element_type=jnp.float32)
    is_odd = lax.broadcasted_iota(jnp.int32, (n, LANES), 0) % 2 == 1
    columns = []
    for face in range(2):
        base = face * (n // BLK_DEV) * ROWS
        for span in range(SPANS):
            rows = []
            for part in range(2):
                direct = got_ref[pl.ds(base + even_row(span) + part, n, stride=ROWS // 2), :]
                start = late_row(span) + part
                shift = 1 if start < ROWS // 2 else 2
                late = got_ref[pl.ds(base + start % (ROWS // 2), n, stride=ROWS // 2), :]
                rows.append(pltpu.roll(direct + jnp.where(is_odd, pltpu.roll(late, n - shift, 0), 0.0), BLK_DEV * TURNS[face], 0))
            columns.append(jnp.concatenate(rows, axis=0))
    force = jnp.concatenate([force_ref[FIRST_FACE], force_ref[1 - FIRST_FACE]], axis=1)
    q_all = jnp.concatenate(columns, axis=1) * force[NC : NC + 1]
    m = 2 * n
    both = dot(jnp.concatenate([q_all, force], axis=0), q_all, NT, precision=HIGH)
    square, load = both[:m], both[m:]
    gram_re = (square[:n, :n] + square[n:, n:]) / total_faces
    gram_im = (square[:n, n:] - square[n:, :n]) / total_faces
    gram = jnp.concatenate(
        [jnp.concatenate([gram_re, -gram_im], axis=1), jnp.concatenate([gram_im, gram_re], axis=1)], axis=0
    )
    load = load / math.sqrt(total_faces * block_count)
    cycle = n // BLK_DEV
    own = cycle * lax.rem(lax.axis_index("face") + FIRST_FACE, 2) + lax.rem(lax.axis_index("blk") + (cycle - TURN), cycle)
    modes = jnp.concatenate([start_ref[0, own], start_ref[1, own]], axis=1)
    columns = [jnp.sum(gram * modes[i : i + 1], axis=1, keepdims=True) for i in range(NMODE)]
    columns = [y / jnp.sqrt(jnp.sum(y * y, axis=0, keepdims=True) / block_count + 1e-06) for y in columns]
    modes = jnp.concatenate([jnp.sum(gram * y, axis=0, keepdims=True) for y in columns], axis=0)
    modes = modes / jnp.sqrt(jnp.sum(modes * modes, axis=1, keepdims=True) / block_count + 1e-06)
    re, im = modes[:, :n], modes[:, n:]
    signed = jnp.concatenate([jnp.concatenate([re, -im], axis=1), jnp.concatenate([im, re], axis=1)], axis=0)
    lane = lax.broadcasted_iota(jnp.int32, (2 * NMODE, LANES), 1)
    line = lax.broadcasted_iota(jnp.int32, (2 * NMODE, LANES), 0)
    tail = jnp.zeros((2 * NMODE, LANES), jnp.float32)
    for c in range(NC):
        answer = jnp.sum(signed * load[c : c + 1], axis=1, keepdims=True)
        tail = jnp.where(lane == F_LANE + 2 * NMODE * c + line, answer, tail)
    tail = jnp.sum(tail, axis=0, keepdims=True)
    lower = jnp.concatenate([gram[n:], jnp.zeros((n, LANES - m), jnp.float32)], axis=1)
    moved = pltpu.roll(lower, m, 1)
    for d in range(cycle):
        reply = lower[2 * d : 2 * d + 1] + moved[2 * d + 1 : 2 * d + 2] + tail
        for face in range(2):
            out_ref[turned(face * cycle + d, -TURN)] = reply


def modes_call(got, force, start, total_faces, block_count):
    vmem = pl.BlockSpec(memory_space=pltpu.VMEM)
    return pl.pallas_call(
        functools.partial(modes_kernel, total_faces, block_count),
        in_specs=[vmem, vmem, vmem],
        out_specs=vmem,
        out_shape=jax.ShapeDtypeStruct((BIN, 1, 128), jnp.float32),
        compiler_params=pltpu.CompilerParams(vmem_limit_bytes=32 * 2**20),
        name="bin_modes",
    )(got, force, start)


def outputs_kernel(block_count, back_ref, gram_ref, forces_ref):
    n = block_count
    back = back_ref[...]
    for part in range(2):
        for row in range(BLK_DEV):
            lane = 2 * n * row + n * (1 - part)
            gram_ref[part, :, row, :] = back[:, lane : lane + n]
    turned = back.T
    for part in range(2):
        for c in range(NC):
            line = F_LANE + 2 * NMODE * c + NMODE * part
            forces_ref[part, c] = turned[line : line + NMODE]


def outputs_call(back, block_count):
    vmem = pl.BlockSpec(memory_space=pltpu.VMEM)
    return pl.pallas_call(
        functools.partial(outputs_kernel, block_count),
        in_specs=[vmem],
        out_specs=[vmem, vmem],
        out_shape=[
            jax.ShapeDtypeStruct((2, BIN, BLK_DEV, block_count), jnp.float32),
            jax.ShapeDtypeStruct((2, NC, NMODE, BIN), jnp.float32),
        ],
        compiler_params=pltpu.CompilerParams(vmem_limit_bytes=16 * 2**20),
        name="outputs",
    )(back)


def by_bins(record, face_area, face_tap, lever_table, start_modes):
    faces = record.shape[1]
    cycle = lax.axis_size("blk")
    block_count = BLK_DEV * cycle
    messages = spectra_call(jnp.asarray(folded_twiddle()), record)
    force = force_call(face_area.reshape(1, faces), face_tap.reshape(1, faces), lever_table.T)
    forces = lax.all_gather(force, "face")
    got = lax.all_to_all(messages, ("face", "blk"), 0, 0, tiled=True, axis_index_groups=spectra_order())
    replies = modes_call(
        got.reshape(BIN * ROWS, LANES), forces, start_modes.transpose(0, 1, 3, 2), faces * 2, block_count
    )
    back = lax.all_to_all(replies, ("face", "blk"), 0, 0, tiled=True, axis_index_groups=order(TURN))
    gram_rows, forces = outputs_call(back.reshape(BIN, 128), block_count)
    return gram_rows, forces.transpose(0, 3, 2, 1)


def shifted(x, axis, by):
    count = lax.axis_size(axis)
    return lax.ppermute(x, axis, [(i, (i + by) % count) for i in range(count)])


def gram_tiles(weighted, others):
    real_tile = jnp.einsum("kif,kjf->kij", weighted[0], others[0], precision=HIGH)
    real_tile = real_tile + jnp.einsum("kif,kjf->kij", weighted[1], others[1], precision=HIGH)
    imag_tile = jnp.einsum("kif,kjf->kij", weighted[0], others[1], precision=HIGH)
    imag_tile = imag_tile - jnp.einsum("kif,kjf->kij", weighted[1], others[0], precision=HIGH)
    return jnp.stack([real_tile, imag_tile])


def by_rows(record, face_area, face_tap, lever_table, start_modes):
    faces = record.shape[1]
    cycle = lax.axis_size("blk")
    block_count = BLK_DEV * cycle
    total_faces = faces * lax.axis_size("face")
    twiddle = jnp.asarray(band_twiddle())
    hops = record.reshape(BLK_DEV, HOP, faces)
    early = jnp.einsum("tk,btf->kbf", twiddle[:HOP], hops, precision=HIGH)
    late = jnp.einsum("tk,btf->kbf", twiddle[HOP:], hops, precision=HIGH)
    following = shifted(late[:, :1], "blk", -1)
    spectra = early + jnp.concatenate([late[:, 1:], following], axis=1)
    panels = jnp.stack([spectra[:BIN], spectra[BIN:]])
    weight = face_area.astype(jnp.float32) / 64.0
    gram_rows = gram_tiles(panels * weight, lax.all_gather(panels, "blk", axis=2, tiled=True))
    gram_rows = lax.psum(gram_rows, "face") / total_faces
    gram = lax.all_gather(gram_rows, "blk", axis=2, tiled=True)
    re, im = start_modes[0], start_modes[1]
    product = functools.partial(jnp.einsum, "kij,kjm->kim", precision=HIGH)
    for _ in range(PITERS):
        re, im = product(gram[0], re) - product(gram[1], im), product(gram[0], im) + product(gram[1], re)
        scale = jnp.sqrt(jnp.sum(re * re + im * im, axis=1, keepdims=True) / block_count + 1e-06)
        re, im = re / scale, im / scale
    own = BLK_DEV * lax.axis_index("blk")
    re = lax.dynamic_slice_in_dim(re, own, BLK_DEV, 1)
    im = lax.dynamic_slice_in_dim(im, own, BLK_DEV, 1)
    onehot = (face_tap[:, None] == jnp.arange(NTAP, dtype=jnp.int32)[None, :]).astype(jnp.float32)
    face_weight = weight[:, None] * jnp.dot(onehot, lever_table.astype(jnp.float32), precision=HIGH)
    load = jnp.einsum("pkbf,fc->pkbc", panels, face_weight, precision=HIGH) / math.sqrt(total_faces * block_count)
    force = functools.partial(jnp.einsum, "kbc,kbm->kmc", precision=HIGH)
    forces = jnp.stack([force(load[0], re) - force(load[1], im), force(load[0], im) + force(load[1], re)])
    return gram_rows, lax.psum(forces, ("blk", "face"))


def solution(mesh):
    fits = mesh.shape["blk"] * mesh.shape["face"] == BIN and mesh.shape["face"] == 2
    return jax.shard_map(
        by_bins if fits else by_rows,
        mesh=mesh,
        in_specs=(P("blk", ("grp", "face")), P("face"), P("face"), P(), P()),
        out_specs=(P(None, "grp", "blk", None), P(None, "grp", None, None)),
        check_vma=False,
    )
```

```python
import functools
import math

import jax
import jax.numpy as jnp
import ml_dtypes
import numpy as np
from jax import lax
from jax.experimental import pallas as pl
from jax.experimental.pallas import tpu as pltpu
from jax.sharding import PartitionSpec as P

NFFT = 1024
HOP = 512
BIN = 16
FIRST_BIN = 24
PITERS = 2
BLK_DEV = 2
NTAP = 512
NMODE = 4
NC = 3
LANES = 128
SPANS = 8
ROWS = 48
SPLIT = 2
F_LANE = 64
VMEM_LIMIT = 60 * 2**20
TURN = 5
FIRST_FACE = 1
TURNS = (5, 2)

HIGH = lax.Precision.HIGHEST
NT = (((1,), (1,)), ((), ()))


def band_twiddle():
    steps = np.arange(NFFT)
    bins = FIRST_BIN + np.arange(BIN)
    angle = (steps[:, None] * bins[None, :] % NFFT) * (2.0 * math.pi / NFFT)
    window = 0.5 - 0.5 * np.cos(steps * (2.0 * math.pi / NFFT))
    scaling = np.sqrt(np.sum(window * window))
    cosine = window[:, None] * np.cos(angle) / scaling
    sine = -window[:, None] * np.sin(angle) / scaling
    return np.concatenate([cosine, sine], axis=1).astype(np.float32)


def thirds(x, cast):
    first = x.astype(jnp.bfloat16)
    rest = x - cast(first)
    second = rest.astype(jnp.bfloat16)
    third = (rest - cast(second)).astype(jnp.bfloat16)
    return first, second, third


def folded_twiddle():
    twiddle = band_twiddle().reshape(2, HOP, 2, BIN)
    rows = twiddle.transpose(0, 3, 2, 1).reshape(4 * BIN, HOP)
    first = rows.astype(ml_dtypes.bfloat16)
    rest = rows - first.astype(np.float32)
    second = rest.astype(ml_dtypes.bfloat16)
    third = (rest - second.astype(np.float32)).astype(ml_dtypes.bfloat16)
    return np.concatenate([first, second, third], axis=0)


def turned(place, by):
    cycle = BIN // 2
    return place // cycle * cycle + (place + by) % cycle


def order(turn):
    return [[(turned(place, turn) + FIRST_FACE * (BIN // 2)) % BIN for place in range(BIN)]]


def spectra_order():
    cycle = BIN // 2
    faces = (FIRST_FACE, 1 - FIRST_FACE)
    return [[faces[half] * cycle + (place + TURNS[half]) % cycle for half in range(2) for place in range(cycle)]]


def f32(x):
    return x.astype(jnp.float32)


def even_row(span):
    return 2 * span


def odd_row(span):
    return ROWS // 2 + 2 * span


def late_row(span):
    return 2 * SPANS + 2 * span if span < SPANS // 2 else ROWS // 2 + SPANS + 2 * span


def spectra_kernel(twiddle_hbm, record_hbm, out_ref, twiddle, record, twiddle_sem, record_sems):
    faces = record.shape[1]
    width = faces // SPLIT
    parts = [slice(q * width, (q + 1) * width) for q in range(SPLIT)]
    small = pltpu.make_async_copy(twiddle_hbm.at[: twiddle.shape[0]], twiddle, twiddle_sem)
    large = [
        pltpu.make_async_copy(record_hbm.at[:, part], record.at[:, part], record_sems.at[q]) for q, part in enumerate(parts)
    ]
    small.start()
    for copy in large:
        copy.start()
    dot = functools.partial(jnp.dot, preferred_element_type=jnp.float32)
    small.wait()
    m = 4 * BIN
    for q, part in enumerate(parts):
        large[q].wait()
        halves = []
        for hop in range(BLK_DEV):
            first, second, third = thirds(record[hop * HOP : (hop + 1) * HOP, part], f32)
            one = dot(twiddle[...], first)
            two = dot(twiddle[: 2 * m], second)
            three = dot(twiddle[:m], third)
            halves.append(((one[2 * m :] + two[m:]) + three) + (one[m : 2 * m] + two[:m]) + one[:m])
        even = halves[0][: 2 * BIN] + halves[1][2 * BIN :]
        odd = halves[1][: 2 * BIN]
        late = halves[0][2 * BIN :]
        for k in range(BIN):
            pair = slice(2 * k, 2 * k + 2)
            slot = turned(k, TURN - TURNS[k // (BIN // 2)])
            for i in range(width // LANES):
                span, lane = q * (width // LANES) + i, slice(i * LANES, (i + 1) * LANES)
                out_ref[slot, even_row(span) : even_row(span) + 2, :] = even[pair, lane]
                out_ref[slot, odd_row(span) : odd_row(span) + 2, :] = odd[pair, lane]
                out_ref[slot, late_row(span) : late_row(span) + 2, :] = late[pair, lane]


def spectra_call(twiddle, record):
    steps, faces = record.shape
    return pl.pallas_call(
        spectra_kernel,
        in_specs=[pl.BlockSpec(memory_space=pl.ANY)] * 2,
        out_specs=pl.BlockSpec(memory_space=pltpu.VMEM),
        out_shape=jax.ShapeDtypeStruct((BIN, ROWS, LANES), jnp.float32),
        scratch_shapes=[
            pltpu.VMEM((12 * BIN, HOP), jnp.bfloat16),
            pltpu.VMEM(record.shape, jnp.float32),
            pltpu.SemaphoreType.DMA,
            pltpu.SemaphoreType.DMA((SPLIT,)),
        ],
        compiler_params=pltpu.CompilerParams(vmem_limit_bytes=VMEM_LIMIT),
        name="band_spectra",
    )(twiddle, record)


def force_kernel(area_ref, tap_ref, lever_ref, out_ref):
    faces = out_ref.shape[1]
    root = jnp.sqrt(f32(area_ref[...]) / 64.0)
    taps = lax.broadcasted_iota(jnp.int32, (NTAP, faces), 0)
    onehot = jnp.where(taps == tap_ref[...], 1.0, 0.0).astype(jnp.bfloat16)
    lever = f32(lever_ref[...]).astype(jnp.bfloat16)
    out_ref[0:NC] = jnp.dot(lever, onehot, preferred_element_type=jnp.float32) * root
    out_ref[NC : NC + 1] = root
    out_ref[NC + 1 :] = jnp.zeros((7 - NC, faces), jnp.float32)


def force_call(area, tap, lever):
    vmem = pl.BlockSpec(memory_space=pltpu.VMEM)
    return pl.pallas_call(
        force_kernel,
        in_specs=[vmem, vmem, vmem],
        out_specs=vmem,
        out_shape=jax.ShapeDtypeStruct((8, area.shape[1]), jnp.float32),
        compiler_params=pltpu.CompilerParams(vmem_limit_bytes=16 * 2**20),
        cost_estimate=pl.CostEstimate(flops=2**21, bytes_accessed=2**16, transcendentals=0),
        name="force_rows",
    )(area, tap, lever)


def modes_kernel(total_faces, block_count, got_ref, force_ref, start_ref, out_ref):
    n = block_count
    dot = functools.partial(lax.dot_general, preferred_element_type=jnp.float32)
    is_odd = lax.broadcasted_iota(jnp.int32, (n, LANES), 0) % 2 == 1
    columns = []
    for face in range(2):
        base = face * (n // BLK_DEV) * ROWS
        for span in range(SPANS):
            rows = []
            for part in range(2):
                direct = got_ref[pl.ds(base + even_row(span) + part, n, stride=ROWS // 2), :]
                start = late_row(span) + part
                shift = 1 if start < ROWS // 2 else 2
                late = got_ref[pl.ds(base + start % (ROWS // 2), n, stride=ROWS // 2), :]
                rows.append(pltpu.roll(direct + jnp.where(is_odd, pltpu.roll(late, n - shift, 0), 0.0), BLK_DEV * TURNS[face], 0))
            columns.append(jnp.concatenate(rows, axis=0))
    force = jnp.concatenate([force_ref[FIRST_FACE], force_ref[1 - FIRST_FACE]], axis=1)
    q_all = jnp.concatenate(columns, axis=1) * force[NC : NC + 1]
    m = 2 * n
    both = dot(jnp.concatenate([q_all, force], axis=0), q_all, NT, precision=HIGH)
    square, load = both[:m], both[m:]
    gram_re = (square[:n, :n] + square[n:, n:]) / total_faces
    gram_im = (square[:n, n:] - square[n:, :n]) / total_faces
    gram = jnp.concatenate(
        [jnp.concatenate([gram_re, -gram_im], axis=1), jnp.concatenate([gram_im, gram_re], axis=1)], axis=0
    )
    load = load / math.sqrt(total_faces * block_count)
    cycle = n // BLK_DEV
    own = cycle * lax.rem(lax.axis_index("face") + FIRST_FACE, 2) + lax.rem(lax.axis_index("blk") + (cycle - TURN), cycle)
    modes = jnp.concatenate([start_ref[0, own], start_ref[1, own]], axis=1)
    columns = [jnp.sum(gram * modes[i : i + 1], axis=1, keepdims=True) for i in range(NMODE)]
    columns = [y / jnp.sqrt(jnp.sum(y * y, axis=0, keepdims=True) / block_count + 1e-06) for y in columns]
    modes = jnp.concatenate([jnp.sum(gram * y, axis=0, keepdims=True) for y in columns], axis=0)
    modes = modes / jnp.sqrt(jnp.sum(modes * modes, axis=1, keepdims=True) / block_count + 1e-06)
    re, im = modes[:, :n], modes[:, n:]
    signed = jnp.concatenate([jnp.concatenate([re, -im], axis=1), jnp.concatenate([im, re], axis=1)], axis=0)
    lane = lax.broadcasted_iota(jnp.int32, (2 * NMODE, LANES), 1)
    line = lax.broadcasted_iota(jnp.int32, (2 * NMODE, LANES), 0)
    tail = jnp.zeros((2 * NMODE, LANES), jnp.float32)
    for c in range(NC):
        answer = jnp.sum(signed * load[c : c + 1], axis=1, keepdims=True)
        tail = jnp.where(lane == F_LANE + 2 * NMODE * c + line, answer, tail)
    tail = jnp.sum(tail, axis=0, keepdims=True)
    lower = jnp.concatenate([gram[n:], jnp.zeros((n, LANES - m), jnp.float32)], axis=1)
    moved = pltpu.roll(lower, m, 1)
    for d in range(cycle):
        reply = lower[2 * d : 2 * d + 1] + moved[2 * d + 1 : 2 * d + 2] + tail
        for face in range(2):
            out_ref[turned(face * cycle + d, -TURN)] = reply


def modes_call(got, force, start, total_faces, block_count):
    vmem = pl.BlockSpec(memory_space=pltpu.VMEM)
    return pl.pallas_call(
        functools.partial(modes_kernel, total_faces, block_count),
        in_specs=[vmem, vmem, vmem],
        out_specs=vmem,
        out_shape=jax.ShapeDtypeStruct((BIN, 1, 128), jnp.float32),
        compiler_params=pltpu.CompilerParams(vmem_limit_bytes=32 * 2**20),
        name="bin_modes",
    )(got, force, start)


def outputs_kernel(block_count, back_ref, gram_ref, forces_ref):
    n = block_count
    back = back_ref[...]
    for part in range(2):
        for row in range(BLK_DEV):
            lane = 2 * n * row + n * (1 - part)
            gram_ref[part, :, row, :] = back[:, lane : lane + n]
    turned = back.T
    for part in range(2):
        for c in range(NC):
            line = F_LANE + 2 * NMODE * c + NMODE * part
            forces_ref[part, c] = turned[line : line + NMODE]


def outputs_call(back, block_count):
    vmem = pl.BlockSpec(memory_space=pltpu.VMEM)
    return pl.pallas_call(
        functools.partial(outputs_kernel, block_count),
        in_specs=[vmem],
        out_specs=[vmem, vmem],
        out_shape=[
            jax.ShapeDtypeStruct((2, BIN, BLK_DEV, block_count), jnp.float32),
            jax.ShapeDtypeStruct((2, NC, NMODE, BIN), jnp.float32),
        ],
        compiler_params=pltpu.CompilerParams(vmem_limit_bytes=16 * 2**20),
        name="outputs",
    )(back)


def by_bins(record, face_area, face_tap, lever_table, start_modes):
    faces = record.shape[1]
    cycle = lax.axis_size("blk")
    block_count = BLK_DEV * cycle
    messages = spectra_call(jnp.asarray(folded_twiddle()), record)
    force = force_call(face_area.reshape(1, faces), face_tap.reshape(1, faces), lever_table.T)
    forces = lax.all_gather(force, "face")
    got = lax.all_to_all(messages, ("face", "blk"), 0, 0, tiled=True, axis_index_groups=spectra_order())
    replies = modes_call(
        got.reshape(BIN * ROWS, LANES), forces, start_modes.transpose(0, 1, 3, 2), faces * 2, block_count
    )
    back = lax.all_to_all(replies, ("face", "blk"), 0, 0, tiled=True, axis_index_groups=order(TURN))
    gram_rows, forces = outputs_call(back.reshape(BIN, 128), block_count)
    return gram_rows, forces.transpose(0, 3, 2, 1)


def shifted(x, axis, by):
    count = lax.axis_size(axis)
    return lax.ppermute(x, axis, [(i, (i + by) % count) for i in range(count)])


def gram_tiles(weighted, others):
    real_tile = jnp.einsum("kif,kjf->kij", weighted[0], others[0], precision=HIGH)
    real_tile = real_tile + jnp.einsum("kif,kjf->kij", weighted[1], others[1], precision=HIGH)
    imag_tile = jnp.einsum("kif,kjf->kij", weighted[0], others[1], precision=HIGH)
    imag_tile = imag_tile - jnp.einsum("kif,kjf->kij", weighted[1], others[0], precision=HIGH)
    return jnp.stack([real_tile, imag_tile])


def by_rows(record, face_area, face_tap, lever_table, start_modes):
    faces = record.shape[1]
    cycle = lax.axis_size("blk")
    block_count = BLK_DEV * cycle
    total_faces = faces * lax.axis_size("face")
    twiddle = jnp.asarray(band_twiddle())
    hops = record.reshape(BLK_DEV, HOP, faces)
    early = jnp.einsum("tk,btf->kbf", twiddle[:HOP], hops, precision=HIGH)
    late = jnp.einsum("tk,btf->kbf", twiddle[HOP:], hops, precision=HIGH)
    following = shifted(late[:, :1], "blk", -1)
    spectra = early + jnp.concatenate([late[:, 1:], following], axis=1)
    panels = jnp.stack([spectra[:BIN], spectra[BIN:]])
    weight = face_area.astype(jnp.float32) / 64.0
    gram_rows = gram_tiles(panels * weight, lax.all_gather(panels, "blk", axis=2, tiled=True))
    gram_rows = lax.psum(gram_rows, "face") / total_faces
    gram = lax.all_gather(gram_rows, "blk", axis=2, tiled=True)
    re, im = start_modes[0], start_modes[1]
    product = functools.partial(jnp.einsum, "kij,kjm->kim", precision=HIGH)
    for _ in range(PITERS):
        re, im = product(gram[0], re) - product(gram[1], im), product(gram[0], im) + product(gram[1], re)
        scale = jnp.sqrt(jnp.sum(re * re + im * im, axis=1, keepdims=True) / block_count + 1e-06)
        re, im = re / scale, im / scale
    own = BLK_DEV * lax.axis_index("blk")
    re = lax.dynamic_slice_in_dim(re, own, BLK_DEV, 1)
    im = lax.dynamic_slice_in_dim(im, own, BLK_DEV, 1)
    onehot = (face_tap[:, None] == jnp.arange(NTAP, dtype=jnp.int32)[None, :]).astype(jnp.float32)
    face_weight = weight[:, None] * jnp.dot(onehot, lever_table.astype(jnp.float32), precision=HIGH)
    load = jnp.einsum("pkbf,fc->pkbc", panels, face_weight, precision=HIGH) / math.sqrt(total_faces * block_count)
    force = functools.partial(jnp.einsum, "kbc,kbm->kmc", precision=HIGH)
    forces = jnp.stack([force(load[0], re) - force(load[1], im), force(load[0], im) + force(load[1], re)])
    return gram_rows, lax.psum(forces, ("blk", "face"))


def solution(mesh):
    fits = mesh.shape["blk"] * mesh.shape["face"] == BIN and mesh.shape["face"] == 2
    return jax.shard_map(
        by_bins if fits else by_rows,
        mesh=mesh,
        in_specs=(P("blk", ("grp", "face")), P("face"), P("face"), P(), P()),
        out_specs=(P(None, "grp", "blk", None), P(None, "grp", None, None)),
        check_vma=False,
    )
```
